512 devices in a mesh: pool: 8 (over z), context: 32 (over x, y), tensor: 2 (over core).
Axes of the slice: x: 4, y: 8, z: 8, core: 2. Of those that a mesh axis runs over, the one named last changes fastest.
Arguments:
- cache: bfloat16 [8, 32, 16, 576], P('pool', 'context'), may hold values from -6 to 6
- hit_slots: int32 [8, 32], P('pool'), may hold values from 0 to 31, each once within a row
- prefix_blocks: int32 [8], P('pool'), may hold values from 10 to 32, as said below
- suffix_len: int32 [8], P('pool'), may hold values from 512 to 2048, as said below
- suffix_latent: bfloat16 [8, 2048, 576], P('pool', 'context')
- suffix_query: bfloat16 [8, 2048, 64, 576], P('pool', 'context', 'tensor')
- decode_hidden: bfloat16 [8, 2, 7168], P('pool'), may hold values from -6 to 6
- kv_down: bfloat16 [7168, 576], P(('context', 'tensor')), may hold values from -0.0625 to 0.0625
- kv_gain: float32 [512], replicated, may hold values from 0.1 to 1.9
- decode_query: bfloat16 [8, 2, 64, 576], P('pool', None, 'tensor')
Outputs:
- suffix_context: bfloat16 [8, 2048, 64, 512], P('pool', 'context', 'tensor')
- decode_context: bfloat16 [8, 2, 64, 512], P('pool', None, 'tensor')
- decode_latent: bfloat16 [8, 2, 576], P('pool')
The draws below stay inside these ranges and needn't reach their ends.
Inputs may be any that keep to these rules, and one draw needn't show every extreme that they name: `prefix_blocks`: some request has all of its group's 32 slots as hits. `suffix_len`: some request has all 2048 suffix tokens valid.
All inputs are finite; a program needn't handle non-finite values.
Results may differ from the reference program's by a relative error of at most 0.03.
Values may be sent and summed in bfloat16 or wider, within the bound.
A program may use at most 128 MiB of HBM per device.

```python
import math
import jax
import jax.numpy as jnp
from jax import lax

D = 7168
H = 64
LAT = 512
ROPE = 64
KVW = 576
BLK = 16
DEC = 2
SUFFIX = 2048
SLOTS = 32
N_POOL = 8


def base_latent(key):
    return jax.random.normal(key, (N_POOL, SUFFIX, KVW), jnp.float32)


def draw_suffix_latent(key, part):
    base = base_latent(key)
    return base.astype(jnp.bfloat16)


def draw_suffix_query(key, part):
    key = jax.random.fold_in(key, 11)
    queries = jax.random.normal(key, (N_POOL, SUFFIX, H, KVW), jnp.float32)
    return queries.astype(jnp.bfloat16)


def draw_decode_query(key, part):
    key = jax.random.fold_in(key, 13)
    queries = jax.random.normal(key, (N_POOL, DEC, H, KVW), jnp.float32)
    return queries.astype(jnp.bfloat16)


def draw_prefix_blocks(key, part):
    key = jax.random.fold_in(key, 21)
    counts = jax.random.randint(key, (N_POOL,), max(1, SLOTS // 3), SLOTS + 1)
    chosen = jax.random.randint(jax.random.fold_in(key, 1), (), 0, N_POOL)
    return jnp.where(jnp.arange(N_POOL) == chosen, SLOTS, counts).astype(jnp.int32)


def draw_suffix_len(key, part):
    key = jax.random.fold_in(key, 23)
    counts = jax.random.randint(key, (N_POOL,), max(1, SUFFIX // 4), SUFFIX + 1)
    chosen = jax.random.randint(jax.random.fold_in(key, 1), (), 0, N_POOL)
    return jnp.where(jnp.arange(N_POOL) == chosen, SUFFIX, counts).astype(jnp.int32)


def steps_of(key, extent, cuts, low, high):
    def one(position, parts):
        heights = jax.random.uniform(jax.random.fold_in(jax.random.fold_in(key, 6), position), (parts,), jnp.float32, low / len(cuts), high / len(cuts))
        return jnp.repeat(jnp.exp(heights), extent[position] // parts).reshape((-1,) + (1,) * (len(extent) - position - 1))

    level = one(*cuts[0])
    for cut in cuts[1:]:
        level = level * one(*cut)
    return level


def scatter_about(stream_key, extent, deviation, limit, shards=(), kind=jnp.bfloat16):
    result = deviation * jax.random.normal(stream_key, extent, jnp.float32)
    if shards:
        result = result * steps_of(stream_key, extent, shards, -0.22, 0.18)
    return jnp.clip(result, -limit, limit).astype(kind)


def setup_inputs(seed: int = 0) -> dict:
    keys = jax.random.split(jax.random.key(seed), 11)
    cache = scatter_about(keys[0], (N_POOL, SLOTS, BLK, KVW), 1.0, 6.0, ((0, 8), (1, 32)))
    hit_slots = jax.vmap(lambda own: jax.random.permutation(own, SLOTS))(jax.random.split(keys[1], N_POOL)).reshape((N_POOL, SLOTS)).astype(jnp.int32)
    prefix_blocks = draw_prefix_blocks(jax.random.fold_in(keys[10], 71), 0)
    suffix_len = draw_suffix_len(jax.random.fold_in(keys[10], 71), 0)
    suffix_latent = draw_suffix_latent(jax.random.fold_in(keys[10], 71), 0)
    suffix_query = draw_suffix_query(jax.random.fold_in(keys[10], 71), 0)
    decode_hidden = scatter_about(keys[6], (N_POOL, DEC, D), 1.0, 6.0, ((0, 8),))
    kv_down = scatter_about(keys[7], (D, KVW), D ** -0.5, 0.0625, ((0, 64),))
    kv_gain = jnp.clip(1.0 + 0.18 * jax.random.normal(keys[8], (LAT,), jnp.float32), 0.1, 1.9)
    decode_query = draw_decode_query(jax.random.fold_in(keys[10], 71), 0)
    return {"cache": cache, "hit_slots": hit_slots, "prefix_blocks": prefix_blocks, "suffix_len": suffix_len, "suffix_latent": suffix_latent, "suffix_query": suffix_query, "decode_hidden": decode_hidden, "kv_down": kv_down, "kv_gain": kv_gain, "decode_query": decode_query}


SCALE = 192.0 ** (-0.5)
NEG = -1e+30

def attend_rows(queries, key_rows, allowed):
    scores = jnp.einsum('rhc,kc->rhk', queries.astype(jnp.float32), key_rows.astype(jnp.float32)) * SCALE
    scores = jnp.where(allowed[:, None, :], scores, NEG)
    top = lax.optimization_barrier(jnp.max(scores, axis=-1, keepdims=True))
    weights = jnp.where(allowed[:, None, :], jnp.exp(scores - top), 0.0).astype(jnp.bfloat16)
    denom = lax.optimization_barrier(jnp.sum(weights.astype(jnp.float32), axis=-1))
    accum = jnp.einsum('rhk,kc->rhc', weights.astype(jnp.float32), key_rows[:, :LAT].astype(jnp.float32))
    return (accum / denom[..., None]).astype(jnp.bfloat16)

def rotate_latent(raw, kv_gain, positions):
    latent = raw[:, :LAT]
    normed = latent * lax.rsqrt(lax.optimization_barrier(jnp.mean(latent * latent, axis=-1, keepdims=True)) + 1e-06) * kv_gain
    half = ROPE // 2
    freq = 10000.0 ** (-jnp.arange(half, dtype=jnp.float32) / half)
    angle = positions[:, None] * freq[None, :]
    first = raw[:, LAT:LAT + half]
    second = raw[:, LAT + half:]
    cosine = jnp.cos(angle)
    sine = jnp.sin(angle)
    rotated = jnp.concatenate([first * cosine - second * sine, second * cosine + first * sine], axis=-1)
    return jnp.concatenate([normed, rotated], axis=-1).astype(jnp.bfloat16)

def reference(cache, hit_slots, prefix_blocks, suffix_len, suffix_latent, suffix_query, decode_hidden, kv_down, kv_gain, decode_query):
    suffix_out = []
    decode_out = []
    latent_out = []
    slot_ids = jnp.arange(SLOTS, dtype=jnp.int32)
    token_ids = jnp.arange(SUFFIX, dtype=jnp.int32)
    dec_ids = jnp.arange(DEC, dtype=jnp.int32)
    qblock = math.gcd(SUFFIX, 64)
    for group in range(N_POOL):
        hits = hit_slots[group]
        slot_live = jnp.any((hits[:, None] == slot_ids[None, :]) & (slot_ids < prefix_blocks[group])[:, None], axis=0)
        cache_rows = cache[group].reshape(SLOTS * BLK, KVW)
        cache_keep = jnp.repeat(slot_live, BLK)
        key_rows = jnp.concatenate([cache_rows, suffix_latent[group]], axis=0)
        group_query = suffix_query[group]

        def one_block(index):
            queries = lax.dynamic_slice_in_dim(group_query, index * qblock, qblock, 0)
            rows = index * qblock + jnp.arange(qblock, dtype=jnp.int32)
            allowed = jnp.concatenate([jnp.broadcast_to(cache_keep[None, :], (qblock, SLOTS * BLK)), token_ids[None, :] <= rows[:, None]], axis=1)
            return attend_rows(queries, key_rows, allowed)
        blocks = lax.map(one_block, jnp.arange(SUFFIX // qblock, dtype=jnp.int32))
        suffix_out.append(blocks.reshape(SUFFIX, H, LAT))
        raw = jnp.dot(decode_hidden[group], kv_down, preferred_element_type=jnp.float32)
        positions = (prefix_blocks[group] * BLK + suffix_len[group] + dec_ids).astype(jnp.float32)
        fresh = rotate_latent(raw, kv_gain, positions)
        latent_out.append(fresh)
        all_rows = jnp.concatenate([key_rows, fresh], axis=0)
        allowed = jnp.concatenate([jnp.broadcast_to(cache_keep[None, :], (DEC, SLOTS * BLK)), jnp.broadcast_to((token_ids < suffix_len[group])[None, :], (DEC, SUFFIX)), dec_ids[None, :] <= dec_ids[:, None]], axis=1)
        decode_out.append(attend_rows(decode_query[group], all_rows, allowed))
    return (jnp.stack(suffix_out), jnp.stack(decode_out), jnp.stack(latent_out))
```

```python
import functools

import jax
import jax.numpy as jnp
from jax import lax
from jax.experimental import pallas as pl
from jax.experimental.pallas import tpu as pltpu
from jax.sharding import PartitionSpec as P

SCALE2 = 192.0 ** (-0.5) * 1.4426950408889634
BIG = -1e38
MESH = pl.DeviceIdType.MESH

NX, NY = 4, 8
TOK, HEADS, KVW, LAT, WIDE = 64, 32, 576, 512, 640
ROWS = TOK * HEADS
DROWS = 2 * HEADS
A_ROWS, B_ROWS = 48, 32
A_GROUP, B_GROUP = NY * A_ROWS, NX * B_ROWS
B_BASE = NX * A_GROUP
KEYS = B_BASE + NY * B_GROUP
QBLK = 512
KSUB = 256


A_STEP = ((0, 48), (48, 96), (144, 96), (240, 96), (336, 48))
B_SUB = ((0, 32), (32, 64), (96, 32))


def a_off(group, row):
    return group * A_GROUP + row


def b_off(group, row):
    return B_BASE + group * B_GROUP + row


def minus(step):
    return 2 * step - 1 if step else 0


def plus(step):
    return 2 * step


def message_plan():
    plan = {}
    for s in (1, 2, 3):
        plan["ayM", s] = (a_off(0, minus(s - 1) * 48), a_off(0, minus(s) * 48), 48, "y+")
        plan["ayP", s] = (a_off(0, plus(s - 1) * 48), a_off(0, plus(s) * 48), 48, "y-")
    plan["ayM", 4] = (a_off(0, minus(3) * 48), a_off(0, 336), 32, "y+")
    plan["ayP", 4] = (a_off(0, plus(3) * 48 + 32), a_off(0, 368), 16, "y-")
    far = (((0, 32), (32, 16)), ((48, 48), (96, 48)), ((144, 48), (192, 48)), ((240, 48), (288, 48)), ((336, 16), (352, 32)))
    for s in range(5):
        row, count = A_STEP[s]
        plan["axM", s] = (a_off(0, row), a_off(1, row), count, "x+")
        plan["axP", s] = (a_off(0, row), a_off(2, row), count, "x-")
        (row_m, count_m), (row_p, count_p) = far[s]
        plan["axxM", s] = (a_off(1, row_m), a_off(3, row_m), count_m, "x+")
        plan["axxP", s] = (a_off(2, row_p), a_off(3, row_p), count_p, "x-")
        for g in range(4):
            if (g, s) != (0, 0):
                plan["as", g, s] = (a_off(g, row), a_off(g, row), count, "core")
    plan["bxM", 1] = (b_off(0, 0), b_off(0, 32), 32, "x+")
    plan["bxP", 1] = (b_off(0, 0), b_off(0, 64), 32, "x-")
    plan["bxM", 2] = (b_off(0, 32), b_off(0, 96), 16, "x+")
    plan["bxP", 2] = (b_off(0, 64 + 16), b_off(0, 96 + 16), 16, "x-")
    halves = (((0, 16), (16, 16)), ((32, 32), (64, 32)), ((96, 16), (112, 16)))
    for u in range(3):
        row, count = B_SUB[u]
        for s in (1, 2, 3):
            plan["byM", s, u] = (b_off(minus(s - 1), row), b_off(minus(s), row), count, "y+")
            plan["byP", s, u] = (b_off(plus(s - 1), row), b_off(plus(s), row), count, "y-")
        (row_m, count_m), (row_p, count_p) = halves[u]
        plan["byM", 4, u] = (b_off(minus(3), row_m), b_off(7, row_m), count_m, "y+")
        plan["byP", 4, u] = (b_off(plus(3), row_p), b_off(7, row_p), count_p, "y-")
        for g in range(8):
            if (g, u) != (0, 0):
                plan["bs", g, u] = (b_off(g, row), b_off(g, row), count, "core")
    return plan


PLAN = message_plan()
INDEX = {name: i for i, name in enumerate(PLAN)}


def events_a():
    out = [("send", ("ayM", 1)), ("send", ("ayP", 1)), ("send", ("axM", 0)), ("send", ("axP", 0)), ("sum",)]

    def near(s):
        out.extend([("wait", ("axM", s)), ("send", ("axxM", s)), ("send", ("as", 1, s))])
        out.extend([("wait", ("axP", s)), ("send", ("axxP", s)), ("send", ("as", 2, s))])

    def far(s):
        out.extend([("wait", ("axxM", s)), ("wait", ("axxP", s)), ("send", ("as", 3, s))])

    for s in (1, 2, 3, 4):
        out.append(("wait", ("ayM", s)))
        if s < 4:
            out.append(("send", ("ayM", s + 1)))
        out.append(("wait", ("ayP", s)))
        if s < 4:
            out.append(("send", ("ayP", s + 1)))
        out.extend([("send", ("axM", s)), ("send", ("axP", s)), ("send", ("as", 0, s))])
        near(s - 1)
        if s >= 2:
            far(s - 2)
        out.append(("sum",))
    near(4)
    out.append(("sum",))
    far(3)
    far(4)
    return out


def events_b():
    out = [("send", ("bxM", 1)), ("send", ("bxP", 1)), ("send", ("byM", 1, 0)), ("send", ("byP", 1, 0)), ("sum",)]
    out.extend([("wait", ("bxM", 1)), ("send", ("bxM", 2)), ("wait", ("bxP", 1)), ("send", ("bxP", 2))])
    out.extend([("send", ("byM", 1, 1)), ("send", ("byP", 1, 1)), ("send", ("bs", 0, 1))])

    def hop(s, u):
        out.append(("wait", ("byM", s, u)))
        if s < 4:
            out.extend([("send", ("byM", s + 1, u)), ("send", ("bs", minus(s), u))])
        out.append(("wait", ("byP", s, u)))
        if s < 4:
            out.extend([("send", ("byP", s + 1, u)), ("send", ("bs", plus(s), u))])
        else:
            out.append(("send", ("bs", 7, u)))

    hop(1, 0)
    out.append(("sum",))
    out.extend([("wait", ("bxM", 2)), ("wait", ("bxP", 2))])
    out.extend([("send", ("byM", 1, 2)), ("send", ("byP", 1, 2)), ("send", ("bs", 0, 2))])
    for diagonal in range(2, 7):
        for u in (2, 1, 0):
            if 1 <= diagonal - u <= 4:
                hop(diagonal - u, u)
        if diagonal < 6:
            out.append(("sum",))
    return out


def gather_kernel(
    hits_ref,
    prefix_ref,
    slen_ref,
    suffix_ref,
    cache_ref,
    hidden_ref,
    down_ref,
    dq_ref,
    q_ref,
    key_ref,
    qa_ref,
    raw_ref,
    q_in,
    part_send,
    part_recv,
    send_sem,
    recv_sem,
    psend_sem,
    precv_sem,
    q_sem,
):
    pool = lax.axis_index("pool")
    ctx = lax.axis_index("context")
    core = lax.axis_index("tensor")
    x, y = ctx // NY, ctx % NY
    x_plus, x_minus = (x + 1) % NX, (x + NX - 1) % NX
    y_plus, y_minus = (y + 1) % NY, (y + NY - 1) % NY
    place = {
        "x+": (pool, x_plus * NY + y, core),
        "x-": (pool, x_minus * NY + y, core),
        "y+": (pool, x * NY + y_plus, core),
        "y-": (pool, x * NY + y_minus, core),
        "core": (pool, ctx, 1 - core),
    }
    x_pair = x + 1 - 2 * (x % 2)
    y_pair = y + 1 - 2 * (y % 2)
    y_four = (y // 4) * 4 + 3 - y % 4
    fold = [
        place["core"],
        (pool, x_pair * NY + y, core),
        (pool, (NX - 1 - x) * NY + y, core),
        (pool, x * NY + y_pair, core),
        (pool, x * NY + y_four, core),
        (pool, x * NY + NY - 1 - y, core),
    ]

    q_copy = pltpu.make_async_copy(q_ref, q_in, q_sem)
    q_copy.start()

    barrier = pltpu.get_barrier_semaphore()
    friends = list(place.values()) + fold[4:]
    for friend in friends:
        pl.semaphore_signal(barrier, inc=1, device_id=friend, device_id_type=MESH)

    prefix = prefix_ref[0]
    slen = slen_ref[0]
    lane = lax.broadcasted_iota(jnp.int32, (TOK, TOK), 1)
    token = lax.broadcasted_iota(jnp.int32, (TOK, TOK), 0) + ctx * TOK
    hidden_here = ((lane < 32) & (ctx > lane)) | ((lane == 32) & (token >= slen))
    tail = jnp.where(hidden_here, BIG, 0.0).astype(jnp.bfloat16)
    own = jnp.concatenate([suffix_ref[...], tail], axis=1)
    order = lax.broadcasted_iota(jnp.int32, (1, 32), 1)
    hit = jnp.where((hits_ref[...] == ctx) & (order < prefix), 1.0, 0.0)
    live = jnp.max(hit, axis=1, keepdims=True)
    dead = jnp.broadcast_to(jnp.where(live > 0.5, 0.0, BIG), (16, TOK)).astype(jnp.bfloat16)
    own_cache = jnp.concatenate([cache_ref[...], dead], axis=1)
    key_ref[0:32, :] = own[0:32]
    key_ref[32:48, :] = own_cache
    key_ref[B_BASE : B_BASE + 32, :] = own[32:64]

    part = ctx * 2 + core
    lane_block = jnp.minimum((part * 112) // 128, 54)
    shift = part * 112 - lane_block * 128
    window = hidden_ref[:, pl.ds(pl.multiple_of(lane_block * 128, 128), 256)]
    pick = lax.broadcasted_iota(jnp.int32, (256, 112), 0) == lax.broadcasted_iota(jnp.int32, (256, 112), 1) + shift
    pick = jnp.where(pick, 1.0, 0.0).astype(jnp.bfloat16)
    piece = jnp.dot(window, pick, preferred_element_type=jnp.float32).astype(jnp.bfloat16)
    partial = jnp.dot(piece, down_ref[...], preferred_element_type=jnp.float32)
    part_send[...] = jnp.zeros_like(part_send)
    part_send[0, 0:2, 0:KVW] = partial

    pl.semaphore_wait(barrier, len(friends))

    def copy_of(name):
        source, target, count, where = PLAN[name]
        i = INDEX[name]
        return pltpu.make_async_remote_copy(
            src_ref=key_ref.at[pl.ds(source, count)],
            dst_ref=key_ref.at[pl.ds(target, count)],
            send_sem=send_sem.at[i],
            recv_sem=recv_sem.at[i],
            device_id=place[where],
            device_id_type=MESH,
        )

    def fold_copy(i):
        return pltpu.make_async_remote_copy(
            src_ref=part_send.at[i],
            dst_ref=part_recv.at[i],
            send_sem=psend_sem.at[i],
            recv_sem=precv_sem.at[i],
            device_id=fold[i],
            device_id_type=MESH,
        )

    def fold_step(i):
        if i > 0:
            fold_copy(i - 1).wait_recv()
            total = part_send[i - 1] + part_recv[i - 1]
            if i < 6:
                part_send[i] = total
            else:
                raw_ref[...] = total
        if i < 6:
            fold_copy(i).start()

    def run(events):
        sums = 0
        for event in events:
            if event[0] == "send":
                copy_of(event[1]).start()
            elif event[0] == "wait":
                copy_of(event[1]).wait_recv()
            else:
                fold_step(sums)
                sums += 1
        return sums

    def sends(events):
        return [event[1] for event in events if event[0] == "send"]

    plan_a, plan_b = events_a(), events_b()

    def side(mine, other):
        done = run(mine)
        q_copy.wait()
        lanes = lax.broadcasted_iota(jnp.int32, (256, TOK), 1)
        pick_rank = jnp.where(lanes == ctx, 1.0, 0.0).astype(jnp.bfloat16)

        def widen(i, carry):
            rows = pl.ds(pl.multiple_of(i * 256, 256), 256)
            qa_ref[rows, :] = jnp.concatenate([q_in[rows, :], pick_rank], axis=1)
            return carry

        lax.fori_loop(0, ROWS // 256, widen, 0)
        pick_dec = jnp.where(lanes[0:DROWS] == 32, 1.0, 0.0).astype(jnp.bfloat16)
        qa_ref[ROWS : ROWS + DROWS, :] = jnp.concatenate([dq_ref[...], pick_dec], axis=1)
        for i in range(done, 7):
            fold_step(i)
        for name in sends(other):
            if PLAN[name][3] == "core":
                copy_of(name).wait_recv()
        for name in sends(mine):
            copy_of(name).wait_send()
        for i in range(6):
            fold_copy(i).wait_send()

    @pl.when(core == 0)
    def _():
        side(plan_a, plan_b)

    @pl.when(core == 1)
    def _():
        side(plan_b, plan_a)


def attend_kernel(
    prefix_ref, slen_ref, key_ref, qa_ref, raw_ref, gain_ref, out_ref, dec_ref, fresh_ref, s0, s1, p0, p1, m_ref, l_ref, o_ref, out_sem
):
    blocks = ROWS // QBLK
    first = [b * QBLK for b in range(blocks)]
    count = [QBLK] * (blocks - 1) + [QBLK + DROWS]
    score, weight = [s0, s1], [p0, p1]
    dims = (((1,), (1,)), ((), ()))
    subs = KEYS // KSUB

    def scores(b, j):
        n = count[b]
        s = lax.dot_general(
            qa_ref[first[b] : first[b] + n, :], key_ref[j * KSUB : (j + 1) * KSUB, :], dims, preferred_element_type=jnp.float32
        )
        base = 0 if j == 0 else (32 if j * KSUB == B_BASE else None)
        if base is not None:
            row = lax.broadcasted_iota(jnp.int32, (n, 128), 0)
            col = lax.broadcasted_iota(jnp.int32, (n, 128), 1)
            tok = (row + first[b]) // HEADS
            mask = (col < 32) & (col + base > tok) & (tok < TOK)
            head = jnp.where(mask, BIG, s[:, 0:128])
            score[b % 2][0:n, j * KSUB : j * KSUB + 128] = head
            score[b % 2][0:n, j * KSUB + 128 : (j + 1) * KSUB] = s[:, 128:]
        else:
            score[b % 2][0:n, j * KSUB : (j + 1) * KSUB] = s

    def row_max(b):
        n = count[b]
        m_ref[b % 2, 0:n] = jnp.max(score[b % 2][0:n, :], axis=1, keepdims=True) * SCALE2

    def soft(b, j, total):
        n = count[b]
        s = score[b % 2][0:n, j * KSUB : (j + 1) * KSUB]
        p = jnp.exp2(s * SCALE2 - m_ref[b % 2, 0:n])
        weight[b % 2][0:n, j * KSUB : (j + 1) * KSUB] = p.astype(jnp.bfloat16)
        return total + jnp.sum(p, axis=1, keepdims=True)

    def fresh_rows():
        raw = raw_ref[...]
        latent = raw[:, 0:LAT]
        norm = latent * lax.rsqrt(jnp.sum(latent * latent, axis=1, keepdims=True) * (1.0 / LAT) + 1e-06) * gain_ref[...]
        tail = raw[:, LAT:WIDE]
        lane = lax.broadcasted_iota(jnp.int32, (8, 128), 1)
        step = lax.broadcasted_iota(jnp.int32, (8, 128), 0)
        pos = (prefix_ref[0] * 16 + slen_ref[0] + step).astype(jnp.float32)
        freq = jnp.exp((lane % 32).astype(jnp.float32) * (-9.210340371976184 / 32.0))
        angle = pos * freq
        cosine, sine = jnp.cos(angle), jnp.sin(angle)
        ahead = pltpu.roll(tail, 96, 1)
        behind = pltpu.roll(tail, 32, 1)
        turned = jnp.where(lane < 32, tail * cosine - ahead * sine, tail * cosine + behind * sine)
        turned = jnp.where(lane < 64, turned, 0.0)
        return jnp.concatenate([norm, turned], axis=1).astype(jnp.bfloat16)

    def context(b):
        n = count[b]
        acc = jnp.dot(weight[b % 2][0:n, :], key_ref[:, 0:LAT], preferred_element_type=jnp.float32)
        total = l_ref[b % 2, 0:n]
        o_ref[first[b] : first[b] + QBLK, :] = (acc[0:QBLK] / total[0:QBLK]).astype(jnp.bfloat16)
        out_copy(b).start()
        if n > QBLK:
            fresh = fresh_rows()
            fresh_ref[...] = fresh[0:2, 0:KVW]
            sf = lax.dot_general(qa_ref[ROWS : ROWS + DROWS, :], fresh, dims, preferred_element_type=jnp.float32) * SCALE2
            row = lax.broadcasted_iota(jnp.int32, (DROWS, 8), 0) // HEADS
            col = lax.broadcasted_iota(jnp.int32, (DROWS, 8), 1)
            sf = jnp.where(col <= row, sf, BIG)
            old = m_ref[b % 2, QBLK:n]
            new = jnp.maximum(old, jnp.max(sf, axis=1, keepdims=True))
            pf = jnp.exp2(sf - new)
            fade = jnp.exp2(old - new)
            total_dec = total[QBLK:n] * fade + jnp.sum(pf, axis=1, keepdims=True)
            more = jnp.dot(pf.astype(jnp.bfloat16), fresh[:, 0:LAT], preferred_element_type=jnp.float32)
            dec_ref[...] = ((acc[QBLK:n] * fade + more) / total_dec).astype(jnp.bfloat16)

    def out_copy(b):
        rows = pl.ds(first[b], QBLK)
        return pltpu.make_async_copy(o_ref.at[rows], out_ref.at[rows], out_sem.at[b])

    for t in range(blocks + 1):
        total = 0.0
        for j in range(subs):
            if t < blocks:
                scores(t, j)
            if t >= 1:
                total = soft(t - 1, j, total)
        if t >= 1:
            l_ref[(t - 1) % 2, 0 : count[t - 1]] = total
            context(t - 1)
        if t < blocks:
            row_max(t)
    for b in range(blocks):
        out_copy(b).wait()


def on_device(
    cache,
    hit_slots,
    prefix_blocks,
    suffix_len,
    suffix_latent,
    suffix_query,
    decode_hidden,
    kv_down,
    kv_gain,
    decode_query,
):
    vmem = pl.BlockSpec(memory_space=pltpu.VMEM)
    smem = pl.BlockSpec(memory_space=pltpu.SMEM)
    anywhere = pl.BlockSpec(memory_space=pl.ANY)
    bf16, f32 = jnp.bfloat16, jnp.float32
    messages = len(PLAN)
    keys, queries, raw = pl.pallas_call(
        gather_kernel,
        name="gather_keys",
        in_specs=[vmem, smem, smem, vmem, vmem, vmem, vmem, vmem, anywhere],
        out_specs=[vmem, vmem, vmem],
        out_shape=[
            pltpu.VMEM((KEYS, WIDE), bf16),
            pltpu.VMEM((ROWS + DROWS, WIDE), bf16),
            pltpu.VMEM((8, WIDE), f32),
        ],
        scratch_shapes=[
            pltpu.VMEM((ROWS, KVW), bf16),
            pltpu.VMEM((6, 8, WIDE), f32),
            pltpu.VMEM((6, 8, WIDE), f32),
            pltpu.SemaphoreType.DMA((messages,)),
            pltpu.SemaphoreType.DMA((messages,)),
            pltpu.SemaphoreType.DMA((6,)),
            pltpu.SemaphoreType.DMA((6,)),
            pltpu.SemaphoreType.DMA,
        ],
        compiler_params=pltpu.CompilerParams(
            collective_id=0, has_side_effects=True, vmem_limit_bytes=24 * 2**20
        ),
    )(
        hit_slots,
        prefix_blocks,
        suffix_len,
        suffix_latent[0],
        cache[0, 0],
        decode_hidden[0],
        kv_down,
        decode_query.reshape(DROWS, KVW),
        suffix_query.reshape(ROWS, KVW),
    )
    tall = QBLK + DROWS
    out, dec, fresh = pl.pallas_call(
        attend_kernel,
        name="attend",
        in_specs=[smem, smem, vmem, vmem, vmem, vmem],
        out_specs=[anywhere, vmem, vmem],
        out_shape=[
            jax.ShapeDtypeStruct((ROWS, LAT), bf16),
            jax.ShapeDtypeStruct((DROWS, LAT), bf16),
            jax.ShapeDtypeStruct((2, KVW), bf16),
        ],
        scratch_shapes=[pltpu.VMEM((tall, KEYS), f32)] * 2
        + [pltpu.VMEM((tall, KEYS), bf16)] * 2
        + [pltpu.VMEM((2, tall, 1), f32)] * 2
        + [pltpu.VMEM((ROWS, LAT), bf16), pltpu.SemaphoreType.DMA((ROWS // QBLK,))],
        compiler_params=pltpu.CompilerParams(vmem_limit_bytes=44 * 2**20),
    )(prefix_blocks, suffix_len, keys, queries, raw, kv_gain.reshape(1, LAT))
    return (
        out.reshape(1, TOK, HEADS, LAT),
        dec.reshape(1, 2, HEADS, LAT),
        fresh.reshape(1, 2, KVW),
    )


def solution(mesh):
    placed = (
        P("pool", "context", None, None),
        P("pool", None),
        P("pool"),
        P("pool"),
        P("pool", "context", None),
        P("pool", "context", "tensor", None),
        P("pool", None, None),
        P(("context", "tensor"), None),
        P(),
        P("pool", None, "tensor", None),
    )
    return jax.shard_map(
        on_device,
        mesh=mesh,
        in_specs=placed,
        out_specs=(
            P("pool", "context", "tensor", None),
            P("pool", None, "tensor", None),
            P("pool", None, None),
        ),
        check_vma=False,
    )
```

```python
import jax
import jax.numpy as jnp
from jax import lax
from jax.experimental import pallas as pl
from jax.experimental.pallas import tpu as pltpu
from jax.sharding import PartitionSpec as P

SCALE2 = 192.0 ** (-0.5) * 1.4426950408889634
BIG = -1e38
MESH = pl.DeviceIdType.MESH
DIMS = (((1,), (1,)), ((), ()))

NX, NY = 4, 8
TOK, HEADS, KVW, LAT, WIDE = 64, 32, 576, 512, 640
ROWS = TOK * HEADS
DROWS = 2 * HEADS
CHUNK = 80
KEYS = NX * NY * CHUNK

SEGMENTS = (
    (0, 0), (0, 1), (1, 0), (2, 0), (0, 2), (3, 0), (1, 1), (2, 1), (0, 3), (0, 4),
    (1, 2), (2, 2), (3, 1), (1, 3), (2, 3), (3, 2), (1, 4), (2, 4), (3, 3), (3, 4),
)


def pair(u):
    return 1 <= u <= 3


def first_chunks():
    place, at = {}, 0
    for g, u in SEGMENTS:
        place[g, u] = at
        at += 2 if pair(u) else 1
    return place


FIRST = first_chunks()
SEM_Y, SEM_X1, SEM_X2, SEM_FAR, SEM_CORE, SEMS = 0, 5, 10, 15, 20, 40

ROW_BLOCKS = ((0, 512), (512, 512), (1024, 512), (1536, 512 + DROWS))
KEY_BLOCKS = ((0, 256), (256, 256), (512, 512), (1024, 512), (1536, 512), (2048, 512))
TALL, BROAD, SUB = 512 + DROWS, 512, 256

SERVICE = {
    (0, 1): (("ready", 2),),
    (0, 3): (("sum",), ("far", 0)),
    (1, 1): (("near", 1), ("ready", 3)),
    (1, 3): (("sum",),),
    (2, 0): (("ready", 4),),
    (2, 1): (("near", 2),),
    (2, 2): (("far", 1),),
    (2, 3): (("sum",),),
    (3, 0): (("near", 3),),
    (3, 1): (("far", 2), ("sum",)),
    (3, 2): (("near", 4),),
    (3, 3): (("sum",),),
    (4, 0): (("far", 3),),
    (4, 1): (("far", 4),),
}


def needed(block):
    start, width = KEY_BLOCKS[block]
    out = []
    for g, u in SEGMENTS:
        low = FIRST[g, u] * CHUNK
        high = low + (2 if pair(u) else 1) * CHUNK
        if low < start + width and high > start:
            out.append((g, u))
    return out


def fused_kernel(
    prefix_ref,
    slen_ref,
    hits_hbm,
    suffix_hbm,
    cache_hbm,
    hidden_hbm,
    down_hbm,
    dq_hbm,
    q_hbm,
    gain_hbm,
    out_ref,
    dec_ref,
    fresh_ref,
    gain_ref,
    hits_ref,
    suffix_ref,
    cache_ref,
    hidden_ref,
    down_ref,
    dq_ref,
    q_in,
    key_ref,
    qa_ref,
    acc_ref,
    m_ref,
    l_ref,
    s0,
    s1,
    p0,
    p1,
    part_send,
    part_recv,
    send_sem,
    recv_sem,
    psend_sem,
    precv_sem,
    in_sem,
):
    pool = lax.axis_index("pool")
    ctx = lax.axis_index("context")
    core = lax.axis_index("tensor")
    x, y = ctx // NY, ctx % NY

    def chip(dx, dy):
        return (pool, ((x + dx + NX) % NX) * NY + (y + dy + NY) % NY, core)

    sister = (pool, ctx, 1 - core)
    along = 1 - 2 * core
    fold = [
        sister,
        (pool, (x + 1 - 2 * (x % 2)) * NY + y, core),
        (pool, (NX - 1 - x) * NY + y, core),
        (pool, x * NY + y + 1 - 2 * (y % 2), core),
        (pool, x * NY + y + 2 - 4 * ((y // 2) % 2), core),
        chip(0, 4),
    ]
    friends = [sister, chip(1, 0), chip(-1, 0), chip(0, 1), chip(0, -1), chip(0, 2), chip(0, -2), chip(0, 4)]
    barrier = pltpu.get_barrier_semaphore()
    for friend in friends:
        pl.semaphore_signal(barrier, inc=1, device_id=friend, device_id_type=MESH)

    loads = (
        (suffix_hbm, suffix_ref),
        (cache_hbm, cache_ref),
        (hits_hbm, hits_ref),
        (hidden_hbm, hidden_ref),
        (down_hbm, down_ref),
        (dq_hbm, dq_ref),
        (q_hbm, q_in),
        (gain_hbm, gain_ref),
    )
    loads = [pltpu.make_async_copy(a, b, in_sem.at[i]) for i, (a, b) in enumerate(loads)]
    for load in loads:
        load.start()

    for load in loads[0:3]:
        load.wait()
    prefix = prefix_ref[0]
    slen = slen_ref[0]
    lane = lax.broadcasted_iota(jnp.int32, (TOK, TOK), 1)
    token = lax.broadcasted_iota(jnp.int32, (TOK, TOK), 0) + ctx * TOK
    hidden_here = ((lane < 32) & (ctx > lane)) | ((lane == 32) & (token >= slen))
    tail = jnp.where(hidden_here, BIG, 0.0).astype(jnp.bfloat16)
    key_ref[0:TOK, :] = jnp.concatenate([suffix_ref[...], tail], axis=1)
    order = lax.broadcasted_iota(jnp.int32, (1, 32), 1)
    hit = jnp.where((hits_ref[...] == ctx) & (order < prefix), 1.0, 0.0)
    live = jnp.max(hit, axis=1, keepdims=True)
    dead = jnp.broadcast_to(jnp.where(live > 0.5, 0.0, BIG), (16, TOK)).astype(jnp.bfloat16)
    key_ref[TOK:CHUNK, :] = jnp.concatenate([cache_ref[...], dead], axis=1)

    for load in loads[3:5]:
        load.wait()
    part = ctx * 2 + core
    lane_block = jnp.minimum((part * 112) // 128, 54)
    shift = part * 112 - lane_block * 128
    window = hidden_ref[:, pl.ds(pl.multiple_of(lane_block * 128, 128), 256)]
    pick = lax.broadcasted_iota(jnp.int32, (256, 112), 0) == lax.broadcasted_iota(jnp.int32, (256, 112), 1) + shift
    pick = jnp.where(pick, 1.0, 0.0).astype(jnp.bfloat16)
    piece = jnp.dot(window, pick, preferred_element_type=jnp.float32).astype(jnp.bfloat16)
    partial = jnp.dot(piece, down_ref[...], preferred_element_type=jnp.float32)
    part_send[...] = jnp.zeros_like(part_send)
    part_send[0, 0:2, 0:KVW] = partial

    pl.semaphore_wait(barrier, len(friends))

    def rows_of(g, u, of_core):
        if pair(u):
            return pl.ds(pl.multiple_of(FIRST[g, u] * CHUNK + of_core * CHUNK, 16), CHUNK)
        return pl.ds(FIRST[g, u] * CHUNK, CHUNK)

    def remote(source, target, i, device, of_core=None):
        of_core = core if of_core is None else of_core
        return pltpu.make_async_remote_copy(
            src_ref=key_ref.at[rows_of(*source, of_core)],
            dst_ref=key_ref.at[rows_of(*target, of_core)],
            send_sem=send_sem.at[i],
            recv_sem=recv_sem.at[i],
            device_id=device,
            device_id_type=MESH,
        )

    def y_copy(u, source, hops):
        return remote((0, source), (0, u), SEM_Y + u, chip(0, along * hops))

    def y_first(u):
        return pltpu.make_async_remote_copy(
            src_ref=key_ref.at[pl.ds(0, CHUNK)],
            dst_ref=key_ref.at[rows_of(0, u, core)],
            send_sem=send_sem.at[SEM_Y + u],
            recv_sem=recv_sem.at[SEM_Y + u],
            device_id=chip(0, along * u),
            device_id_type=MESH,
        )

    def x1_copy(u):
        return remote((0, u), (1, u), SEM_X1 + u, chip(1, 0))

    def x2_copy(u):
        return remote((0, u), (2, u), SEM_X2 + u, chip(-1, 0))

    def far_copy(u):
        if u % 2 == 0:
            return remote((1, u), (3, u), SEM_FAR + u, chip(1, 0))
        return remote((2, u), (3, u), SEM_FAR + u, chip(-1, 0))

    def core_copy(g, u, of_core=None):
        return remote((g, u), (g, u), SEM_CORE + g * 5 + u, sister, of_core)

    def carried(u, action):
        if u == 0:
            pl.when(core == 1)(action)
        elif u == 4:
            pl.when(core == 0)(action)
        else:
            action()

    def y_wait(u):
        if u == 4:
            return y_copy(4, 2, 2)
        if u == 3:
            return y_copy(3, 1, 2)
        return y_first(u)

    def ready(u):
        if u > 0:
            carried(u, lambda: y_wait(u).wait_recv())
        if u == 1:
            y_copy(3, 1, 2).start()
        if u == 2:
            pl.when(core == 0)(lambda: y_copy(4, 2, 2).start())

        def send():
            x1_copy(u).start()
            x2_copy(u).start()
            if u > 0:
                core_copy(0, u).start()

        carried(u, send)

    def near(u):
        def pass_on():
            x1_copy(u).wait_recv()
            if u % 2 == 0:
                far_copy(u).start()
            core_copy(1, u).start()
            x2_copy(u).wait_recv()
            if u % 2 == 1:
                far_copy(u).start()
            core_copy(2, u).start()

        carried(u, pass_on)

    def far(u):
        def pass_on():
            far_copy(u).wait_recv()
            core_copy(3, u).start()

        carried(u, pass_on)

    def fold_copy(i):
        return pltpu.make_async_remote_copy(
            src_ref=part_send.at[i],
            dst_ref=part_recv.at[i],
            send_sem=psend_sem.at[i],
            recv_sem=precv_sem.at[i],
            device_id=fold[i],
            device_id_type=MESH,
        )

    def fold_step(i):
        if i > 0:
            fold_copy(i - 1).wait_recv()
            part_send[i] = part_send[i - 1] + part_recv[i - 1]
        if i < 6:
            fold_copy(i).start()

    sums = [0]
    arrived = {(0, 0)}
    served = {(0, 0)}

    def serve(event):
        kind = event[0]
        if kind == "sum":
            fold_step(sums[0])
            sums[0] += 1
        elif kind == "ready":
            ready(event[1])
            served.add((0, event[1]))
        elif kind == "near":
            near(event[1])
            served.update({(1, event[1]), (2, event[1])})
        else:
            far(event[1])
            served.add((3, event[1]))

    def from_sister(g, u):
        def wait():
            core_copy(g, u, 1 - core).wait_recv()

        if u == 0:
            pl.when(core == 0)(wait)
        elif u == 4:
            pl.when(core == 1)(wait)
        else:
            wait()

    def await_block(block):
        for segment in needed(block):
            if segment not in arrived:
                assert segment in served, segment
                from_sister(*segment)
                arrived.add(segment)

    units = [(k, r) for k in range(len(KEY_BLOCKS)) for r in range(len(ROW_BLOCKS))]
    score, weight = [s0, s1], [p0, p1]
    last = len(KEY_BLOCKS) - 1

    def scores(i, j):
        k, r = units[i]
        start, n = ROW_BLOCKS[r]
        low = KEY_BLOCKS[k][0] + j * SUB
        s = lax.dot_general(qa_ref[start : start + n, :], key_ref[low : low + SUB, :], DIMS, preferred_element_type=jnp.float32)
        if low == 0:
            row = lax.broadcasted_iota(jnp.int32, (n, 128), 0)
            col = lax.broadcasted_iota(jnp.int32, (n, 128), 1)
            tok = (row + start) // HEADS
            mask = (col < TOK) & (col > tok) & (tok < TOK)
            score[i % 2][0:n, 0:128] = jnp.where(mask, BIG, s[:, 0:128])
            score[i % 2][0:n, 128:SUB] = s[:, 128:]
        else:
            score[i % 2][0:n, j * SUB : (j + 1) * SUB] = s

    def subs(i):
        return range(KEY_BLOCKS[units[i][0]][1] // SUB)

    def row_max(i):
        k, r = units[i]
        start, n = ROW_BLOCKS[r]
        top = jnp.max(score[i % 2][0:n, 0 : KEY_BLOCKS[k][1]], axis=1, keepdims=True) * SCALE2
        if k == 0:
            m_ref[start : start + n] = top
            return None
        old = m_ref[start : start + n]
        new = jnp.maximum(old, top)
        m_ref[start : start + n] = new
        return jnp.exp2(old - new)

    def soft(i, j, total):
        k, r = units[i]
        start, n = ROW_BLOCKS[r]
        s = score[i % 2][0:n, j * SUB : (j + 1) * SUB]
        p = jnp.exp2(s * SCALE2 - m_ref[start : start + n])
        weight[i % 2][0:n, j * SUB : (j + 1) * SUB] = p.astype(jnp.bfloat16)
        return total + jnp.sum(p, axis=1, keepdims=True)

    def fresh_rows():
        raw = part_send[6]
        latent = raw[:, 0:LAT]
        norm = latent * lax.rsqrt(jnp.sum(latent * latent, axis=1, keepdims=True) * (1.0 / LAT) + 1e-06) * gain_ref[...]
        rope = raw[:, LAT:WIDE]
        lanes = lax.broadcasted_iota(jnp.int32, (8, 128), 1)
        step = lax.broadcasted_iota(jnp.int32, (8, 128), 0)
        pos = (prefix * 16 + slen + step).astype(jnp.float32)
        freq = jnp.exp((lanes % 32).astype(jnp.float32) * (-9.210340371976184 / 32.0))
        angle = pos * freq
        cosine, sine = jnp.cos(angle), jnp.sin(angle)
        ahead = pltpu.roll(rope, 96, 1)
        behind = pltpu.roll(rope, 32, 1)
        turned = jnp.where(lanes < 32, rope * cosine - ahead * sine, rope * cosine + behind * sine)
        turned = jnp.where(lanes < 64, turned, 0.0)
        return jnp.concatenate([norm, turned], axis=1).astype(jnp.bfloat16)

    def decode_end(acc, total):
        fresh = fresh_rows()
        fresh_ref[...] = fresh[0:2, 0:KVW]
        sf = lax.dot_general(qa_ref[ROWS : ROWS + DROWS, :], fresh, DIMS, preferred_element_type=jnp.float32) * SCALE2
        row = lax.broadcasted_iota(jnp.int32, (DROWS, 8), 0) // HEADS
        col = lax.broadcasted_iota(jnp.int32, (DROWS, 8), 1)
        sf = jnp.where(col <= row, sf, BIG)
        old = m_ref[ROWS : ROWS + DROWS]
        new = jnp.maximum(old, jnp.max(sf, axis=1, keepdims=True))
        pf = jnp.exp2(sf - new)
        fade = jnp.exp2(old - new)
        total = total * fade + jnp.sum(pf, axis=1, keepdims=True)
        more = jnp.dot(pf.astype(jnp.bfloat16), fresh[:, 0:LAT], preferred_element_type=jnp.float32)
        dec_ref[...] = ((acc * fade + more) / total).astype(jnp.bfloat16)

    def context(i, total, fade):
        k, r = units[i]
        start, n = ROW_BLOCKS[r]
        low, width = KEY_BLOCKS[k]
        o = jnp.dot(weight[i % 2][0:n, 0:width], key_ref[low : low + width, 0:LAT], preferred_element_type=jnp.float32)
        here = slice(start, start + n)
        if k > 0:
            total = l_ref[here] * fade + total
            o = acc_ref[here] * fade + o
        if k < last:
            l_ref[here] = total
            acc_ref[here] = o
            return
        end = min(start + n, ROWS) - start
        out_ref[start : start + end, :] = (o[0:end] / total[0:end]).astype(jnp.bfloat16)
        if end < n:
            decode_end(o[end:n], total[end:n])

    y_first(1).start()
    pl.when(core == 0)(lambda: y_first(2).start())

    def own_step():
        pltpu.make_async_remote_copy(
            src_ref=key_ref.at[pl.ds(0, CHUNK)],
            dst_ref=key_ref.at[rows_of(0, 2, core)],
            send_sem=send_sem.at[SEM_Y + 2],
            recv_sem=recv_sem.at[SEM_Y + 2],
            device_id=chip(0, -2),
            device_id_type=MESH,
        ).start()

    pl.when(core == 1)(own_step)
    ready(0)
    serve(("sum",))

    for load in loads[5:]:
        load.wait()
    lanes = lax.broadcasted_iota(jnp.int32, (256, TOK), 1)
    pick_rank = jnp.where(lanes == ctx, 1.0, 0.0).astype(jnp.bfloat16)

    def widen(i, carry):
        rows = pl.ds(pl.multiple_of(i * 256, 256), 256)
        qa_ref[rows, :] = jnp.concatenate([q_in[rows, :], pick_rank], axis=1)
        return carry

    lax.fori_loop(0, ROWS // 256, widen, 0)
    pick_dec = jnp.where(lanes[0:DROWS] == 32, 1.0, 0.0).astype(jnp.bfloat16)
    qa_ref[ROWS : ROWS + DROWS, :] = jnp.concatenate([dq_ref[...], pick_dec], axis=1)

    for event in (("ready", 1), ("near", 0), ("sum",)):
        serve(event)

    await_block(0)
    for j in subs(0):
        scores(0, j)
    fade = row_max(0)
    for i, unit in enumerate(units):
        more = i + 1 < len(units)
        if more and units[i + 1][0] != unit[0]:
            await_block(units[i + 1][0])
        total = 0.0
        ahead = list(subs(i + 1)) if more else []
        for j in range(max(len(ahead), len(subs(i)))):
            if j < len(ahead):
                scores(i + 1, j)
            if j < len(subs(i)):
                total = soft(i, j, total)
        context(i, total, fade)
        if more:
            fade = row_max(i + 1)
        for event in SERVICE.get(unit, ()):
            serve(event)

    assert sums[0] == 7
    y_first(1).wait_send()
    y_copy(3, 1, 2).wait_send()
    y_first(2).wait_send()
    pl.when(core == 0)(lambda: y_copy(4, 2, 2).wait_send())
    for u in range(5):

        def sent(u=u):
            for copy in (x1_copy(u), x2_copy(u), far_copy(u)):
                copy.wait_send()
            for g in range(4):
                if (g, u) != (0, 0):
                    core_copy(g, u).wait_send()

        carried(u, sent)
    for i in range(6):
        fold_copy(i).wait_send()


def on_device(
    cache,
    hit_slots,
    prefix_blocks,
    suffix_len,
    suffix_latent,
    suffix_query,
    decode_hidden,
    kv_down,
    kv_gain,
    decode_query,
):
    vmem = pl.BlockSpec(memory_space=pltpu.VMEM)
    smem = pl.BlockSpec(memory_space=pltpu.SMEM)
    hbm = pl.BlockSpec(memory_space=pltpu.HBM)
    bf16, f32 = jnp.bfloat16, jnp.float32
    out, dec, fresh = pl.pallas_call(
        fused_kernel,
        name="attend",
        in_specs=[smem, smem] + [hbm] * 8,
        out_specs=[vmem, vmem, vmem],
        out_shape=[
            pltpu.VMEM((ROWS, LAT), bf16),
            pltpu.VMEM((DROWS, LAT), bf16),
            pltpu.VMEM((2, KVW), bf16),
        ],
        scratch_shapes=[
            pltpu.VMEM((1, LAT), f32),
            pltpu.VMEM((1, 32), jnp.int32),
            pltpu.VMEM((TOK, KVW), bf16),
            pltpu.VMEM((16, KVW), bf16),
            pltpu.VMEM((2, 7168), bf16),
            pltpu.VMEM((112, KVW), bf16),
            pltpu.VMEM((DROWS, KVW), bf16),
            pltpu.VMEM((ROWS, KVW), bf16),
            pltpu.VMEM((KEYS, WIDE), bf16),
            pltpu.VMEM((ROWS + DROWS, WIDE), bf16),
            pltpu.VMEM((ROWS + DROWS, LAT), f32),
            pltpu.VMEM((ROWS + DROWS, 1), f32),
            pltpu.VMEM((ROWS + DROWS, 1), f32),
            pltpu.VMEM((TALL, BROAD), f32),
            pltpu.VMEM((TALL, BROAD), f32),
            pltpu.VMEM((TALL, BROAD), bf16),
            pltpu.VMEM((TALL, BROAD), bf16),
            pltpu.VMEM((7, 8, WIDE), f32),
            pltpu.VMEM((6, 8, WIDE), f32),
            pltpu.SemaphoreType.DMA((SEMS,)),
            pltpu.SemaphoreType.DMA((SEMS,)),
            pltpu.SemaphoreType.DMA((6,)),
            pltpu.SemaphoreType.DMA((6,)),
            pltpu.SemaphoreType.DMA((8,)),
        ],
        compiler_params=pltpu.CompilerParams(
            collective_id=0, has_side_effects=True, vmem_limit_bytes=48 * 2**20
        ),
    )(
        prefix_blocks,
        suffix_len,
        *(
            pltpu.with_memory_space_constraint(array, pltpu.HBM)
            for array in (
                hit_slots,
                suffix_latent[0],
                cache[0, 0],
                decode_hidden[0],
                kv_down,
                decode_query.reshape(DROWS, KVW),
                suffix_query.reshape(ROWS, KVW),
                kv_gain.reshape(1, LAT),
            )
        ),
    )
    return (
        out.reshape(1, TOK, HEADS, LAT),
        dec.reshape(1, 2, HEADS, LAT),
        fresh.reshape(1, 2, KVW),
    )


def solution(mesh):
    placed = (
        P("pool", "context", None, None),
        P("pool", None),
        P("pool"),
        P("pool"),
        P("pool", "context", None),
        P("pool", "context", "tensor", None),
        P("pool", None, None),
        P(("context", "tensor"), None),
        P(),
        P("pool", None, "tensor", None),
    )
    return jax.shard_map(
        on_device,
        mesh=mesh,
        in_specs=placed,
        out_specs=(
            P("pool", "context", "tensor", None),
            P("pool", None, "tensor", None),
            P("pool", None, None),
        ),
        check_vma=False,
    )
```

```python
import jax
import jax.numpy as jnp
from jax import lax
from jax.experimental import pallas as pl
from jax.experimental.pallas import tpu as pltpu
from jax.sharding import PartitionSpec as P

SCALE2 = 192.0 ** (-0.5) * 1.4426950408889634
BIG = -1e38
MESH = pl.DeviceIdType.MESH
DIMS = (((1,), (1,)), ((), ()))

NX, NY = 4, 8
TOK, HEADS, KVW, LAT, WIDE = 64, 32, 576, 512, 640
ROWS = TOK * HEADS
DROWS = 2 * HEADS
CHUNK = 80
KEYS = NX * NY * CHUNK

SEGMENTS = (
    (0, 0), (0, 1), (1, 0), (2, 0), (0, 2), (3, 0), (1, 1), (2, 1), (0, 3), (0, 4),
    (1, 2), (2, 2), (3, 1), (3, 2), (1, 3), (2, 3), (3, 3), (1, 4), (2, 4), (3, 4),
)
CARRIER = {(0, 4): 0, (1, 4): 0, (2, 4): 0, (3, 4): 0, (1, 0): 0, (2, 0): 1, (3, 0): 0, (3, 1): 0}


def pair(u):
    return 1 <= u <= 3


def first_chunks():
    place, at = {}, 0
    for g, u in SEGMENTS:
        place[g, u] = at
        at += 2 if pair(u) else 1
    return place


FIRST = first_chunks()
SEM_Y, SEM_X1, SEM_X2, SEM_FAR, SEM_CORE, SEM_SIDE, SEMS = 0, 5, 10, 15, 20, 40, 42

ROW_BLOCKS = ((0, 512), (512, 512), (1024, 512), (1536, 512 + DROWS))
KEY_BLOCKS = ((0, 256), (256, 256), (512, 512), (1024, 512), (1536, 512), (2048, 256), (2304, 256))
TALL, BROAD, SUB = 512 + DROWS, 512, 256

SERVICE = {
    (0, 1): (("ready", 2),),
    (0, 3): (("far", 0),),
    (1, 0): (("sum",),),
    (1, 1): (("ready", 3), ("near", 1)),
    (2, 0): (("ready", 4), ("near", 2)),
    (2, 1): (("side",), ("sum",)),
    (2, 3): (("sum",),),
    (3, 1): (("far", 2),),
    (3, 2): (("near", 3), ("far", 3)),
    (3, 3): (("sum",),),
    (4, 0): (("near", 4), ("far", 4)),
    (4, 3): (("sum",),),
}


def needed(block):
    start, width = KEY_BLOCKS[block]
    out = []
    for g, u in SEGMENTS:
        low = FIRST[g, u] * CHUNK
        high = low + (2 if pair(u) else 1) * CHUNK
        if low < start + width and high > start:
            out.append((g, u))
    return out


def fused_kernel(
    prefix_ref,
    slen_ref,
    hits_hbm,
    suffix_hbm,
    cache_hbm,
    hidden_hbm,
    down_hbm,
    dq_hbm,
    q_hbm,
    gain_hbm,
    out_ref,
    dec_ref,
    fresh_ref,
    gain_ref,
    hits_ref,
    suffix_ref,
    cache_ref,
    hidden_ref,
    down_ref,
    dq_ref,
    q_in,
    key_ref,
    qa_ref,
    acc_ref,
    m_ref,
    l_ref,
    s0,
    s1,
    p0,
    p1,
    part_send,
    part_recv,
    send_sem,
    recv_sem,
    psend_sem,
    precv_sem,
    in_sem,
):
    pool = lax.axis_index("pool")
    ctx = lax.axis_index("context")
    core = lax.axis_index("tensor")
    x, y = ctx // NY, ctx % NY

    def chip(dx, dy):
        return (pool, ((x + dx + NX) % NX) * NY + (y + dy + NY) % NY, core)

    sister = (pool, ctx, 1 - core)
    along = 1 - 2 * core
    fold = [
        sister,
        (pool, (x + 1 - 2 * (x % 2)) * NY + y, core),
        (pool, (NX - 1 - x) * NY + y, core),
        (pool, x * NY + y + 1 - 2 * (y % 2), core),
        (pool, x * NY + y + 2 - 4 * ((y // 2) % 2), core),
        chip(0, 4),
    ]
    friends = [sister, chip(1, 0), chip(-1, 0), chip(2, 0), chip(0, 1), chip(0, -1), chip(0, 2), chip(0, -2), chip(0, 4)]
    barrier = pltpu.get_barrier_semaphore()
    for friend in friends:
        pl.semaphore_signal(barrier, inc=1, device_id=friend, device_id_type=MESH)

    loads = (
        (suffix_hbm, suffix_ref),
        (cache_hbm, cache_ref),
        (hits_hbm, hits_ref),
        (hidden_hbm, hidden_ref),
        (down_hbm, down_ref),
        (dq_hbm, dq_ref),
        (q_hbm, q_in),
        (gain_hbm, gain_ref),
    )
    loads = [pltpu.make_async_copy(a, b, in_sem.at[i]) for i, (a, b) in enumerate(loads)]
    for load in loads:
        load.start()

    for load in loads[0:3]:
        load.wait()
    prefix = prefix_ref[0]
    slen = slen_ref[0]
    lane = lax.broadcasted_iota(jnp.int32, (TOK, TOK), 1)
    token = lax.broadcasted_iota(jnp.int32, (TOK, TOK), 0) + ctx * TOK
    hidden_here = ((lane < 32) & (ctx > lane)) | ((lane == 32) & (token >= slen))
    tail = jnp.where(hidden_here, BIG, 0.0).astype(jnp.bfloat16)
    key_ref[0:TOK, :] = jnp.concatenate([suffix_ref[...], tail], axis=1)
    order = lax.broadcasted_iota(jnp.int32, (1, 32), 1)
    hit = jnp.where((hits_ref[...] == ctx) & (order < prefix), 1.0, 0.0)
    live = jnp.max(hit, axis=1, keepdims=True)
    dead = jnp.broadcast_to(jnp.where(live > 0.5, 0.0, BIG), (16, TOK)).astype(jnp.bfloat16)
    key_ref[TOK:CHUNK, :] = jnp.concatenate([cache_ref[...], dead], axis=1)

    pl.semaphore_wait(barrier, len(friends))

    def rows_of(g, u, of_core):
        if pair(u):
            return pl.ds(pl.multiple_of(FIRST[g, u] * CHUNK + of_core * CHUNK, 16), CHUNK)
        return pl.ds(FIRST[g, u] * CHUNK, CHUNK)

    def span(g, u):
        return pl.ds(FIRST[g, u] * CHUNK, 2 * CHUNK if pair(u) else CHUNK)

    def remote(source, target, i, device):
        return pltpu.make_async_remote_copy(
            src_ref=key_ref.at[source],
            dst_ref=key_ref.at[target],
            send_sem=send_sem.at[i],
            recv_sem=recv_sem.at[i],
            device_id=device,
            device_id_type=MESH,
        )

    def y_copy(u):
        source, hops = (rows_of(0, 0, core), u) if u <= 2 else (rows_of(0, u - 2, core), 2)
        return remote(source, rows_of(0, u, core), SEM_Y + u, chip(0, along * hops))

    def near_copy(g, u):
        base = SEM_X1 if g == 1 else SEM_X2
        return remote(rows_of(0, u, core), rows_of(g, u, core), base + u, chip(1 if g == 1 else -1, 0))

    def far_copy(u):
        if u == 0:
            source, hops = rows_of(1, 0, core), 1
        elif u == 2:
            source, hops = rows_of(2, 2, core), -1
        else:
            source, hops = rows_of(0, u, core), 2
        return remote(source, rows_of(3, u, core), SEM_FAR + u, chip(hops, 0))

    def side_copy(way):
        return remote(rows_of(3, 0, core), rows_of(3, 1, way), SEM_SIDE + way, chip(0, 1 - 2 * way))

    def core_copy(g, u, of_core=None):
        if (g, u) in CARRIER or not pair(u):
            rows = span(g, u)
        else:
            rows = rows_of(g, u, core if of_core is None else of_core)
        return remote(rows, rows, SEM_CORE + g * 5 + u, sister)

    def on(which, action):
        if which is None:
            action()
        else:
            pl.when(core == which)(action)

    started = []

    def launch(which, *copies):
        def start():
            for make in copies:
                make().start()

        on(which, start)
        started.append((which, copies))

    def take(g, u, *copies):
        which = CARRIER.get((g, u))

        def wait():
            for make in copies:
                make().wait_recv()

        on(which, wait)
        return which

    def ready(u):
        which = take(0, u, lambda: y_copy(u))
        if u == 1:
            launch(which, lambda: y_copy(3))
        if u == 2:
            launch(0, lambda: y_copy(4))
        launch(which, lambda: near_copy(1, u), lambda: near_copy(2, u))
        if u >= 3:
            launch(which, lambda: far_copy(u))
        launch(which, lambda: core_copy(0, u))

    def near(u):
        for g in (1, 2):
            which = take(g, u, lambda g=g: near_copy(g, u))
            if u == 0 and g == 1:
                launch(which, lambda: far_copy(0))
            if u == 2 and g == 2:
                launch(which, lambda: far_copy(2))
            launch(which, lambda g=g: core_copy(g, u))

    def far(u):
        which = take(3, u, lambda: far_copy(u))
        if u == 0:
            launch(which, lambda: side_copy(0), lambda: side_copy(1))
        launch(which, lambda: core_copy(3, u))

    def side():
        which = take(3, 1, lambda: side_copy(0), lambda: side_copy(1))
        launch(which, lambda: core_copy(3, 1))

    def fold_copy(i):
        return pltpu.make_async_remote_copy(
            src_ref=part_send.at[i],
            dst_ref=part_recv.at[i],
            send_sem=psend_sem.at[i],
            recv_sem=precv_sem.at[i],
            device_id=fold[i],
            device_id_type=MESH,
        )

    def fold_step(i):
        if i > 0:
            fold_copy(i - 1).wait_recv()
            part_send[i] = part_send[i - 1] + part_recv[i - 1]
        if i < 6:
            fold_copy(i).start()

    sums = [0]
    arrived = {(0, 0)}
    served = {(0, 0)}

    def serve(event):
        kind = event[0]
        if kind == "sum":
            fold_step(sums[0])
            sums[0] += 1
        elif kind == "ready":
            ready(event[1])
            served.add((0, event[1]))
        elif kind == "near":
            near(event[1])
            served.update({(1, event[1]), (2, event[1])})
        elif kind == "far":
            far(event[1])
            served.add((3, event[1]))
        else:
            side()
            served.add((3, 1))

    def from_sister(g, u):
        which = CARRIER.get((g, u))
        on(None if which is None else 1 - which, lambda: core_copy(g, u, 1 - core).wait_recv())

    def await_block(block):
        for segment in needed(block):
            if segment not in arrived:
                assert segment in served, segment
                from_sister(*segment)
                arrived.add(segment)

    units = [(k, r) for k in range(len(KEY_BLOCKS)) for r in range(len(ROW_BLOCKS))]
    score, weight = [s0, s1], [p0, p1]
    last = len(KEY_BLOCKS) - 1

    def wide(state, lanes):
        return jnp.concatenate([state] * (lanes // 128), axis=1)

    def scores(i, j):
        k, r = units[i]
        start, n = ROW_BLOCKS[r]
        low = KEY_BLOCKS[k][0] + j * SUB
        s = lax.dot_general(qa_ref[start : start + n, :], key_ref[low : low + SUB, :], DIMS, preferred_element_type=jnp.float32)
        if low == 0:
            row = lax.broadcasted_iota(jnp.int32, (n, 128), 0)
            col = lax.broadcasted_iota(jnp.int32, (n, 128), 1)
            tok = (row + start) // HEADS
            mask = (col < TOK) & (col > tok) & (tok < TOK)
            score[i % 2][0:n, 0:128] = jnp.where(mask, BIG, s[:, 0:128])
            score[i % 2][0:n, 128:SUB] = s[:, 128:]
        else:
            score[i % 2][0:n, j * SUB : (j + 1) * SUB] = s

    def subs(i):
        return range(KEY_BLOCKS[units[i][0]][1] // SUB)

    def row_max(i):
        k, r = units[i]
        start, n = ROW_BLOCKS[r]
        top = jnp.max(score[i % 2][0:n, 0 : KEY_BLOCKS[k][1]], axis=1, keepdims=True) * SCALE2
        top = jnp.broadcast_to(top, (n, 128))
        if k == 0:
            m_ref[start : start + n] = top
            return None
        old = m_ref[start : start + n]
        new = jnp.maximum(old, top)
        m_ref[start : start + n] = new
        return jnp.exp2(old - new)

    def soft(i, j, total):
        k, r = units[i]
        start, n = ROW_BLOCKS[r]
        s = score[i % 2][0:n, j * SUB : (j + 1) * SUB]
        p = jnp.exp2(s * SCALE2 - wide(m_ref[start : start + n], SUB))
        weight[i % 2][0:n, j * SUB : (j + 1) * SUB] = p.astype(jnp.bfloat16)
        for c in range(0, SUB, 128):
            total = p[:, c : c + 128] if total is None else total + p[:, c : c + 128]
        return total

    def fresh_rows():
        raw = part_send[6]
        latent = raw[:, 0:LAT]
        norm = latent * lax.rsqrt(jnp.sum(latent * latent, axis=1, keepdims=True) * (1.0 / LAT) + 1e-06) * gain_ref[...]
        rope = raw[:, LAT:WIDE]
        lanes = lax.broadcasted_iota(jnp.int32, (8, 128), 1)
        step = lax.broadcasted_iota(jnp.int32, (8, 128), 0)
        pos = (prefix * 16 + slen + step).astype(jnp.float32)
        freq = jnp.exp((lanes % 32).astype(jnp.float32) * (-9.210340371976184 / 32.0))
        angle = pos * freq
        cosine, sine = jnp.cos(angle), jnp.sin(angle)
        ahead = pltpu.roll(rope, 96, 1)
        behind = pltpu.roll(rope, 32, 1)
        turned = jnp.where(lanes < 32, rope * cosine - ahead * sine, rope * cosine + behind * sine)
        turned = jnp.where(lanes < 64, turned, 0.0)
        return jnp.concatenate([norm, turned], axis=1).astype(jnp.bfloat16)

    def decode_end(acc, total):
        fresh = fresh_rows()
        fresh_ref[...] = fresh[0:2, 0:KVW]
        sf = lax.dot_general(qa_ref[ROWS : ROWS + DROWS, :], fresh, DIMS, preferred_element_type=jnp.float32) * SCALE2
        row = lax.broadcasted_iota(jnp.int32, (DROWS, 8), 0) // HEADS
        col = lax.broadcasted_iota(jnp.int32, (DROWS, 8), 1)
        sf = jnp.where(col <= row, sf, BIG)
        old = m_ref[ROWS : ROWS + DROWS, 0:1]
        new = jnp.maximum(old, jnp.max(sf, axis=1, keepdims=True))
        pf = jnp.exp2(sf - new)
        fade = jnp.exp2(old - new)
        total = total * fade + jnp.sum(pf, axis=1, keepdims=True)
        more = jnp.dot(pf.astype(jnp.bfloat16), fresh[:, 0:LAT], preferred_element_type=jnp.float32)
        dec_ref[...] = ((acc * fade + more) / total).astype(jnp.bfloat16)

    def context(i, total, fade):
        k, r = units[i]
        start, n = ROW_BLOCKS[r]
        low, width = KEY_BLOCKS[k]
        o = jnp.dot(weight[i % 2][0:n, 0:width], key_ref[low : low + width, 0:LAT], preferred_element_type=jnp.float32)
        here = slice(start, start + n)
        if k > 0:
            total = l_ref[here] * fade + total
            o = acc_ref[here] * wide(fade, LAT) + o
        if k < last:
            l_ref[here] = total
            acc_ref[here] = o
            return
        end = min(start + n, ROWS) - start
        total = jnp.sum(total, axis=1, keepdims=True)
        over = jnp.broadcast_to(1.0 / total[0:end], (end, 128))
        out_ref[start : start + end, :] = (o[0:end] * wide(over, LAT)).astype(jnp.bfloat16)
        if end < n:
            decode_end(o[end:n], total[end:n])

    y_copy(1).start()
    launch(0, lambda: near_copy(1, 0))
    launch(1, lambda: near_copy(2, 0))

    for load in loads[3:5]:
        load.wait()
    part = ctx * 2 + core
    lane_block = jnp.minimum((part * 112) // 128, 54)
    shift = part * 112 - lane_block * 128
    window = hidden_ref[:, pl.ds(pl.multiple_of(lane_block * 128, 128), 256)]
    pick = lax.broadcasted_iota(jnp.int32, (256, 112), 0) == lax.broadcasted_iota(jnp.int32, (256, 112), 1) + shift
    pick = jnp.where(pick, 1.0, 0.0).astype(jnp.bfloat16)
    piece = jnp.dot(window, pick, preferred_element_type=jnp.float32).astype(jnp.bfloat16)
    partial = jnp.dot(piece, down_ref[...], preferred_element_type=jnp.float32)
    part_send[...] = jnp.zeros_like(part_send)
    part_send[0, 0:2, 0:KVW] = partial
    y_copy(1).wait_send()
    launch(None, lambda: y_copy(2))
    serve(("sum",))

    for load in loads[5:]:
        load.wait()
    lanes = lax.broadcasted_iota(jnp.int32, (256, TOK), 1)
    pick_rank = jnp.where(lanes == ctx, 1.0, 0.0).astype(jnp.bfloat16)

    def widen(i, carry):
        rows = pl.ds(pl.multiple_of(i * 256, 256), 256)
        qa_ref[rows, :] = jnp.concatenate([q_in[rows, :], pick_rank], axis=1)
        return carry

    lax.fori_loop(0, ROWS // 256, widen, 0)
    pick_dec = jnp.where(lanes[0:DROWS] == 32, 1.0, 0.0).astype(jnp.bfloat16)
    qa_ref[ROWS : ROWS + DROWS, :] = jnp.concatenate([dq_ref[...], pick_dec], axis=1)

    for event in (("ready", 1), ("near", 0), ("sum",)):
        serve(event)

    await_block(0)
    for j in subs(0):
        scores(0, j)
    fade = row_max(0)
    for i, unit in enumerate(units):
        more = i + 1 < len(units)
        if more and units[i + 1][0] != unit[0]:
            await_block(units[i + 1][0])
        total = None
        ahead = list(subs(i + 1)) if more else []
        for j in range(max(len(ahead), len(subs(i)))):
            if j < len(ahead):
                scores(i + 1, j)
            if j < len(subs(i)):
                total = soft(i, j, total)
        context(i, total, fade)
        if more:
            fade = row_max(i + 1)
        for event in SERVICE.get(unit, ()):
            serve(event)

    assert sums[0] == 7
    for which, copies in started:

        def sent(copies=copies):
            for make in copies:
                make().wait_send()

        on(which, sent)
    for i in range(6):
        fold_copy(i).wait_send()


def write_kernel(out_vmem, dec_vmem, fresh_vmem, out_ref, dec_ref, fresh_ref, sem):
    copies = ((out_vmem, out_ref), (dec_vmem, dec_ref), (fresh_vmem, fresh_ref))
    copies = [pltpu.make_async_copy(a, b, sem.at[i]) for i, (a, b) in enumerate(copies)]
    for copy in copies:
        copy.start()
    for copy in copies:
        copy.wait()


def on_device(
    cache,
    hit_slots,
    prefix_blocks,
    suffix_len,
    suffix_latent,
    suffix_query,
    decode_hidden,
    kv_down,
    kv_gain,
    decode_query,
):
    vmem = pl.BlockSpec(memory_space=pltpu.VMEM)
    smem = pl.BlockSpec(memory_space=pltpu.SMEM)
    hbm = pl.BlockSpec(memory_space=pltpu.HBM)
    bf16, f32 = jnp.bfloat16, jnp.float32
    out, dec, fresh = pl.pallas_call(
        fused_kernel,
        name="attend",
        in_specs=[smem, smem] + [hbm] * 8,
        out_specs=[vmem, vmem, vmem],
        out_shape=[
            pltpu.VMEM((ROWS, LAT), bf16),
            pltpu.VMEM((DROWS, LAT), bf16),
            pltpu.VMEM((2, KVW), bf16),
        ],
        scratch_shapes=[
            pltpu.VMEM((1, LAT), f32),
            pltpu.VMEM((1, 32), jnp.int32),
            pltpu.VMEM((TOK, KVW), bf16),
            pltpu.VMEM((16, KVW), bf16),
            pltpu.VMEM((2, 7168), bf16),
            pltpu.VMEM((112, KVW), bf16),
            pltpu.VMEM((DROWS, KVW), bf16),
            pltpu.VMEM((ROWS, KVW), bf16),
            pltpu.VMEM((KEYS, WIDE), bf16),
            pltpu.VMEM((ROWS + DROWS, WIDE), bf16),
            pltpu.VMEM((ROWS + DROWS, LAT), f32),
            pltpu.VMEM((ROWS + DROWS, 128), f32),
            pltpu.VMEM((ROWS + DROWS, 128), f32),
            pltpu.VMEM((TALL, BROAD), f32),
            pltpu.VMEM((TALL, BROAD), f32),
            pltpu.VMEM((TALL, BROAD), bf16),
            pltpu.VMEM((TALL, BROAD), bf16),
            pltpu.VMEM((7, 8, WIDE), f32),
            pltpu.VMEM((6, 8, WIDE), f32),
            pltpu.SemaphoreType.DMA((SEMS,)),
            pltpu.SemaphoreType.DMA((SEMS,)),
            pltpu.SemaphoreType.DMA((6,)),
            pltpu.SemaphoreType.DMA((6,)),
            pltpu.SemaphoreType.DMA((8,)),
        ],
        compiler_params=pltpu.CompilerParams(
            collective_id=0, has_side_effects=True, vmem_limit_bytes=48 * 2**20
        ),
    )(
        prefix_blocks,
        suffix_len,
        *(
            pltpu.with_memory_space_constraint(array, pltpu.HBM)
            for array in (
                hit_slots,
                suffix_latent[0],
                cache[0, 0],
                decode_hidden[0],
                kv_down,
                decode_query.reshape(DROWS, KVW),
                suffix_query.reshape(ROWS, KVW),
                kv_gain.reshape(1, LAT),
            )
        ),
    )
    out, dec, fresh = pl.pallas_call(
        write_kernel,
        name="write",
        in_specs=[vmem] * 3,
        out_specs=[hbm] * 3,
        out_shape=[
            jax.ShapeDtypeStruct((ROWS, LAT), bf16),
            jax.ShapeDtypeStruct((DROWS, LAT), bf16),
            jax.ShapeDtypeStruct((2, KVW), bf16),
        ],
        scratch_shapes=[pltpu.SemaphoreType.DMA((3,))],
    )(out, dec, fresh)
    return (
        out.reshape(1, TOK, HEADS, LAT),
        dec.reshape(1, 2, HEADS, LAT),
        fresh.reshape(1, 2, KVW),
    )


def solution(mesh):
    placed = (
        P("pool", "context", None, None),
        P("pool", None),
        P("pool"),
        P("pool"),
        P("pool", "context", None),
        P("pool", "context", "tensor", None),
        P("pool", None, None),
        P(("context", "tensor"), None),
        P(),
        P("pool", None, "tensor", None),
    )
    return jax.shard_map(
        on_device,
        mesh=mesh,
        in_specs=placed,
        out_specs=(
            P("pool", "context", "tensor", None),
            P("pool", None, "tensor", None),
            P("pool", None, None),
        ),
        check_vma=False,
    )
```

```python
import jax
import jax.numpy as jnp
from jax import lax
from jax.experimental import pallas as pl
from jax.experimental.pallas import tpu as pltpu
from jax.sharding import PartitionSpec as P

SCALE2 = 192.0 ** (-0.5) * 1.4426950408889634
BIG = -1e38
MESH = pl.DeviceIdType.MESH
DIMS = (((1,), (1,)), ((), ()))

NX, NY = 4, 8
TOK, HEADS, KVW, LAT, WIDE = 64, 32, 576, 512, 640
ROWS = TOK * HEADS
DROWS = 2 * HEADS
CHUNK = 80
KEYS = NX * NY * CHUNK

SEGMENTS = (
    (0, 0), (0, 1), (1, 0), (2, 0), (0, 2), (3, 0), (1, 1), (2, 1), (0, 3), (0, 4),
    (1, 2), (2, 2), (3, 1), (3, 2), (1, 3), (2, 3), (1, 4), (2, 4), (3, 3), (3, 4),
)
CARRIER = {(0, 4): 0, (1, 4): 0, (2, 4): 0, (3, 4): 0, (1, 0): 0, (2, 0): 1, (3, 0): 0, (3, 1): 0}


def pair(u):
    return 1 <= u <= 3


def first_chunks():
    place, at = {}, 0
    for g, u in SEGMENTS:
        place[g, u] = at
        at += 2 if pair(u) else 1
    return place


FIRST = first_chunks()
SEM_Y, SEM_X1, SEM_X2, SEM_FAR, SEM_CORE, SEM_SIDE, SEMS = 0, 5, 10, 15, 20, 40, 42

ROW_BLOCKS = ((0, 512), (512, 512), (1024, 512), (1536, 512 + DROWS))
KEY_BLOCKS = ((0, 256), (256, 256), (512, 512), (1024, 512), (1536, 512), (2048, 256), (2304, 256))
TALL, BROAD, SUB = 512 + DROWS, 512, 256

SERVICE = {
    (0, 2): (("sum",), ("ready", 2)),
    (0, 3): (("far", 0),),
    (1, 0): (("near", 1), ("ready", 3)),
    (1, 2): (("near", 2),),
    (2, 0): (("side",), ("sum",), ("ready", 4)),
    (2, 2): (("near", 3),),
    (3, 0): (("far", 2), ("sum",)),
    (3, 2): (("near", 4),),
    (4, 1): (("far", 3), ("sum",)),
    (4, 2): (("far", 4),),
    (6, 0): (("sum",),),
}


def needed(block):
    start, width = KEY_BLOCKS[block]
    out = []
    for g, u in SEGMENTS:
        low = FIRST[g, u] * CHUNK
        high = low + (2 if pair(u) else 1) * CHUNK
        if low < start + width and high > start:
            out.append((g, u))
    return out


def fused_kernel(
    prefix_ref,
    slen_ref,
    hits_hbm,
    suffix_hbm,
    cache_hbm,
    hidden_hbm,
    down_hbm,
    dq_hbm,
    q_hbm,
    gain_hbm,
    out_ref,
    dec_ref,
    fresh_ref,
    gain_ref,
    hits_ref,
    suffix_ref,
    cache_ref,
    hidden_ref,
    down_ref,
    dq_ref,
    q_in,
    key_ref,
    qa_ref,
    acc_ref,
    m_ref,
    l_ref,
    s0,
    s1,
    p0,
    p1,
    part_send,
    part_recv,
    send_sem,
    recv_sem,
    psend_sem,
    precv_sem,
    in_sem,
):
    pool = lax.axis_index("pool")
    ctx = lax.axis_index("context")
    core = lax.axis_index("tensor")
    x, y = ctx // NY, ctx % NY

    def chip(dx, dy):
        return (pool, ((x + dx + NX) % NX) * NY + (y + dy + NY) % NY, core)

    sister = (pool, ctx, 1 - core)
    along = 1 - 2 * core
    fold = [
        sister,
        (pool, (x + 1 - 2 * (x % 2)) * NY + y, core),
        (pool, (NX - 1 - x) * NY + y, core),
        (pool, x * NY + y + 1 - 2 * (y % 2), core),
        (pool, x * NY + y + 2 - 4 * ((y // 2) % 2), core),
        chip(0, 4),
    ]
    friends = [sister, chip(1, 0), chip(-1, 0), chip(2, 0), chip(0, 1), chip(0, -1), chip(0, 2), chip(0, -2), chip(0, 4)]
    barrier = pltpu.get_barrier_semaphore()
    for friend in friends:
        pl.semaphore_signal(barrier, inc=1, device_id=friend, device_id_type=MESH)

    loads = (
        (suffix_hbm, suffix_ref),
        (cache_hbm, cache_ref),
        (hits_hbm, hits_ref),
        (hidden_hbm, hidden_ref),
        (down_hbm, down_ref),
        (dq_hbm, dq_ref),
        (q_hbm, q_in),
        (gain_hbm, gain_ref),
    )
    loads = [pltpu.make_async_copy(a, b, in_sem.at[i]) for i, (a, b) in enumerate(loads)]
    for load in loads:
        load.start()

    for load in loads[0:3]:
        load.wait()
    prefix = prefix_ref[0]
    slen = slen_ref[0]
    lane = lax.broadcasted_iota(jnp.int32, (TOK, TOK), 1)
    token = lax.broadcasted_iota(jnp.int32, (TOK, TOK), 0) + ctx * TOK
    hidden_here = ((lane < 32) & (ctx > lane)) | ((lane == 32) & (token >= slen))
    tail = jnp.where(hidden_here, BIG, 0.0).astype(jnp.bfloat16)
    key_ref[0:TOK, :] = jnp.concatenate([suffix_ref[...], tail], axis=1)
    order = lax.broadcasted_iota(jnp.int32, (1, 32), 1)
    hit = jnp.where((hits_ref[...] == ctx) & (order < prefix), 1.0, 0.0)
    live = jnp.max(hit, axis=1, keepdims=True)
    dead = jnp.broadcast_to(jnp.where(live > 0.5, 0.0, BIG), (16, TOK)).astype(jnp.bfloat16)
    key_ref[TOK:CHUNK, :] = jnp.concatenate([cache_ref[...], dead], axis=1)

    pl.semaphore_wait(barrier, len(friends))

    def rows_of(g, u, of_core):
        if pair(u):
            return pl.ds(pl.multiple_of(FIRST[g, u] * CHUNK + of_core * CHUNK, 16), CHUNK)
        return pl.ds(FIRST[g, u] * CHUNK, CHUNK)

    def span(g, u):
        return pl.ds(FIRST[g, u] * CHUNK, 2 * CHUNK if pair(u) else CHUNK)

    def remote(source, target, i, device):
        return pltpu.make_async_remote_copy(
            src_ref=key_ref.at[source],
            dst_ref=key_ref.at[target],
            send_sem=send_sem.at[i],
            recv_sem=recv_sem.at[i],
            device_id=device,
            device_id_type=MESH,
        )

    def y_copy(u):
        source, hops = (rows_of(0, 0, core), u) if u <= 2 else (rows_of(0, u - 2, core), 2)
        return remote(source, rows_of(0, u, core), SEM_Y + u, chip(0, along * hops))

    def near_copy(g, u):
        base = SEM_X1 if g == 1 else SEM_X2
        return remote(rows_of(0, u, core), rows_of(g, u, core), base + u, chip(1 if g == 1 else -1, 0))

    def far_copy(u):
        if u == 0:
            source, hops = rows_of(1, 0, core), 1
        elif u == 2:
            source, hops = rows_of(1, 2, core), 1
        elif u == 3:
            source, hops = rows_of(2, 3, core), -1
        else:
            source, hops = rows_of(0, u, core), 2
        return remote(source, rows_of(3, u, core), SEM_FAR + u, chip(hops, 0))

    def side_copy(way):
        return remote(rows_of(3, 0, core), rows_of(3, 1, way), SEM_SIDE + way, chip(0, 1 - 2 * way))

    def core_copy(g, u, of_core=None):
        if (g, u) in CARRIER or not pair(u):
            rows = span(g, u)
        else:
            rows = rows_of(g, u, core if of_core is None else of_core)
        return remote(rows, rows, SEM_CORE + g * 5 + u, sister)

    def on(which, action):
        if which is None:
            action()
        else:
            pl.when(core == which)(action)

    started = []

    def launch(which, *copies):
        def start():
            for make in copies:
                make().start()

        on(which, start)
        started.append((which, copies))

    def take(g, u, *copies):
        which = CARRIER.get((g, u))

        def wait():
            for make in copies:
                make().wait_recv()

        on(which, wait)
        return which

    def ready(u):
        which = take(0, u, lambda: y_copy(u))
        if u == 1:
            launch(which, lambda: y_copy(3))
        if u == 2:
            launch(0, lambda: y_copy(4))
        launch(which, lambda: near_copy(1, u), lambda: near_copy(2, u))
        if u == 4:
            launch(which, lambda: far_copy(u))
        launch(which, lambda: core_copy(0, u))

    def near(u):
        for g in (1, 2):
            which = take(g, u, lambda g=g: near_copy(g, u))
            if (u, g) in ((0, 1), (2, 1), (3, 2)):
                launch(which, lambda: far_copy(u))
            launch(which, lambda g=g: core_copy(g, u))

    def far(u):
        which = take(3, u, lambda: far_copy(u))
        if u == 0:
            launch(which, lambda: side_copy(0), lambda: side_copy(1))
        launch(which, lambda: core_copy(3, u))

    def side():
        which = take(3, 1, lambda: side_copy(0), lambda: side_copy(1))
        launch(which, lambda: core_copy(3, 1))

    def fold_copy(i):
        return pltpu.make_async_remote_copy(
            src_ref=part_send.at[i],
            dst_ref=part_recv.at[i],
            send_sem=psend_sem.at[i],
            recv_sem=precv_sem.at[i],
            device_id=fold[i],
            device_id_type=MESH,
        )

    def fold_step(i):
        if i > 0:
            fold_copy(i - 1).wait_recv()
            part_send[i] = part_send[i - 1] + part_recv[i - 1]
        if i < 6:
            fold_copy(i).start()

    sums = [0]
    arrived = {(0, 0)}
    served = {(0, 0)}

    def serve(event):
        kind = event[0]
        if kind == "sum":
            fold_step(sums[0])
            sums[0] += 1
        elif kind == "ready":
            ready(event[1])
            served.add((0, event[1]))
        elif kind == "near":
            near(event[1])
            served.update({(1, event[1]), (2, event[1])})
        elif kind == "far":
            far(event[1])
            served.add((3, event[1]))
        else:
            side()
            served.add((3, 1))

    def from_sister(g, u):
        which = CARRIER.get((g, u))
        on(None if which is None else 1 - which, lambda: core_copy(g, u, 1 - core).wait_recv())

    def await_block(block):
        for segment in needed(block):
            if segment not in arrived:
                assert segment in served, segment
                from_sister(*segment)
                arrived.add(segment)

    units = [(k, r) for k in range(len(KEY_BLOCKS)) for r in range(len(ROW_BLOCKS))]
    score, weight = [s0, s1], [p0, p1]
    last = len(KEY_BLOCKS) - 1

    def wide(state, lanes):
        return jnp.concatenate([state] * (lanes // 128), axis=1)

    def scores(i, j):
        k, r = units[i]
        start, n = ROW_BLOCKS[r]
        low = KEY_BLOCKS[k][0] + j * SUB
        s = lax.dot_general(qa_ref[start : start + n, :], key_ref[low : low + SUB, :], DIMS, preferred_element_type=jnp.float32)
        if low == 0:
            row = lax.broadcasted_iota(jnp.int32, (n, 128), 0)
            col = lax.broadcasted_iota(jnp.int32, (n, 128), 1)
            tok = (row + start) // HEADS
            mask = (col < TOK) & (col > tok) & (tok < TOK)
            score[i % 2][0:n, 0:128] = jnp.where(mask, BIG, s[:, 0:128])
            score[i % 2][0:n, 128:SUB] = s[:, 128:]
        else:
            score[i % 2][0:n, j * SUB : (j + 1) * SUB] = s

    def subs(i):
        return range(KEY_BLOCKS[units[i][0]][1] // SUB)

    def row_max(i):
        k, r = units[i]
        start, n = ROW_BLOCKS[r]
        top = jnp.max(score[i % 2][0:n, 0 : KEY_BLOCKS[k][1]], axis=1, keepdims=True) * SCALE2
        top = jnp.broadcast_to(top, (n, 128))
        if k == 0:
            m_ref[start : start + n] = top
            return None
        old = m_ref[start : start + n]
        new = jnp.maximum(old, top)
        m_ref[start : start + n] = new
        return jnp.exp2(old - new)

    def soft(i, j, total):
        k, r = units[i]
        start, n = ROW_BLOCKS[r]
        s = score[i % 2][0:n, j * SUB : (j + 1) * SUB]
        p = jnp.exp2(s * SCALE2 - wide(m_ref[start : start + n], SUB))
        weight[i % 2][0:n, j * SUB : (j + 1) * SUB] = p.astype(jnp.bfloat16)
        for c in range(0, SUB, 128):
            total = p[:, c : c + 128] if total is None else total + p[:, c : c + 128]
        return total

    def fresh_rows():
        raw = part_send[6]
        latent = raw[:, 0:LAT]
        norm = latent * lax.rsqrt(jnp.sum(latent * latent, axis=1, keepdims=True) * (1.0 / LAT) + 1e-06) * gain_ref[...]
        rope = raw[:, LAT:WIDE]
        lanes = lax.broadcasted_iota(jnp.int32, (8, 128), 1)
        step = lax.broadcasted_iota(jnp.int32, (8, 128), 0)
        pos = (prefix * 16 + slen + step).astype(jnp.float32)
        freq = jnp.exp((lanes % 32).astype(jnp.float32) * (-9.210340371976184 / 32.0))
        angle = pos * freq
        cosine, sine = jnp.cos(angle), jnp.sin(angle)
        ahead = pltpu.roll(rope, 96, 1)
        behind = pltpu.roll(rope, 32, 1)
        turned = jnp.where(lanes < 32, rope * cosine - ahead * sine, rope * cosine + behind * sine)
        turned = jnp.where(lanes < 64, turned, 0.0)
        return jnp.concatenate([norm, turned], axis=1).astype(jnp.bfloat16)

    def decode_end(acc, total):
        fresh = fresh_rows()
        fresh_ref[...] = fresh[0:2, 0:KVW]
        sf = lax.dot_general(qa_ref[ROWS : ROWS + DROWS, :], fresh, DIMS, preferred_element_type=jnp.float32) * SCALE2
        row = lax.broadcasted_iota(jnp.int32, (DROWS, 8), 0) // HEADS
        col = lax.broadcasted_iota(jnp.int32, (DROWS, 8), 1)
        sf = jnp.where(col <= row, sf, BIG)
        old = m_ref[ROWS : ROWS + DROWS, 0:1]
        new = jnp.maximum(old, jnp.max(sf, axis=1, keepdims=True))
        pf = jnp.exp2(sf - new)
        fade = jnp.exp2(old - new)
        total = total * fade + jnp.sum(pf, axis=1, keepdims=True)
        more = jnp.dot(pf.astype(jnp.bfloat16), fresh[:, 0:LAT], preferred_element_type=jnp.float32)
        dec_ref[...] = ((acc * fade + more) / total).astype(jnp.bfloat16)

    def context(i, total, fade):
        k, r = units[i]
        start, n = ROW_BLOCKS[r]
        low, width = KEY_BLOCKS[k]
        o = jnp.dot(weight[i % 2][0:n, 0:width], key_ref[low : low + width, 0:LAT], preferred_element_type=jnp.float32)
        here = slice(start, start + n)
        if k > 0:
            total = l_ref[here] * fade + total
            o = acc_ref[here] * wide(fade, LAT) + o
        if k < last:
            l_ref[here] = total
            acc_ref[here] = o
            return
        end = min(start + n, ROWS) - start
        total = jnp.sum(total, axis=1, keepdims=True)
        over = jnp.broadcast_to(1.0 / total[0:end], (end, 128))
        out_ref[start : start + end, :] = (o[0:end] * wide(over, LAT)).astype(jnp.bfloat16)
        if end < n:
            decode_end(o[end:n], total[end:n])

    y_copy(1).start()
    launch(0, lambda: near_copy(1, 0))
    launch(1, lambda: near_copy(2, 0))

    for load in loads[3:5]:
        load.wait()
    part = ctx * 2 + core
    lane_block = jnp.minimum((part * 112) // 128, 54)
    shift = part * 112 - lane_block * 128
    window = hidden_ref[:, pl.ds(pl.multiple_of(lane_block * 128, 128), 256)]
    pick = lax.broadcasted_iota(jnp.int32, (256, 112), 0) == lax.broadcasted_iota(jnp.int32, (256, 112), 1) + shift
    pick = jnp.where(pick, 1.0, 0.0).astype(jnp.bfloat16)
    piece = jnp.dot(window, pick, preferred_element_type=jnp.float32).astype(jnp.bfloat16)
    partial = jnp.dot(piece, down_ref[...], preferred_element_type=jnp.float32)
    part_send[...] = jnp.zeros_like(part_send)
    part_send[0, 0:2, 0:KVW] = partial
    y_copy(1).wait_send()
    launch(None, lambda: y_copy(2))
    serve(("sum",))

    for load in loads[5:]:
        load.wait()
    lanes = lax.broadcasted_iota(jnp.int32, (256, TOK), 1)
    pick_rank = jnp.where(lanes == ctx, 1.0, 0.0).astype(jnp.bfloat16)

    def widen(i, carry):
        rows = pl.ds(pl.multiple_of(i * 256, 256), 256)
        qa_ref[rows, :] = jnp.concatenate([q_in[rows, :], pick_rank], axis=1)
        return carry

    lax.fori_loop(0, ROWS // 256, widen, 0)
    pick_dec = jnp.where(lanes[0:DROWS] == 32, 1.0, 0.0).astype(jnp.bfloat16)
    qa_ref[ROWS : ROWS + DROWS, :] = jnp.concatenate([dq_ref[...], pick_dec], axis=1)

    for event in (("ready", 1), ("near", 0), ("sum",)):
        serve(event)

    await_block(0)
    for j in subs(0):
        scores(0, j)
    fade = row_max(0)
    for i, unit in enumerate(units):
        more = i + 1 < len(units)
        if more and units[i + 1][0] != unit[0]:
            await_block(units[i + 1][0])
        total = None
        ahead = list(subs(i + 1)) if more else []
        for j in range(max(len(ahead), len(subs(i)))):
            if j < len(ahead):
                scores(i + 1, j)
            if j < len(subs(i)):
                total = soft(i, j, total)
        context(i, total, fade)
        if more:
            fade = row_max(i + 1)
        for event in SERVICE.get(unit, ()):
            serve(event)

    assert sums[0] == 7
    for which, copies in started:

        def sent(copies=copies):
            for make in copies:
                make().wait_send()

        on(which, sent)
    for i in range(6):
        fold_copy(i).wait_send()


def write_kernel(out_vmem, dec_vmem, fresh_vmem, out_ref, dec_ref, fresh_ref, sem):
    copies = ((out_vmem, out_ref), (dec_vmem, dec_ref), (fresh_vmem, fresh_ref))
    copies = [pltpu.make_async_copy(a, b, sem.at[i]) for i, (a, b) in enumerate(copies)]
    for copy in copies:
        copy.start()
    for copy in copies:
        copy.wait()


def on_device(
    cache,
    hit_slots,
    prefix_blocks,
    suffix_len,
    suffix_latent,
    suffix_query,
    decode_hidden,
    kv_down,
    kv_gain,
    decode_query,
):
    vmem = pl.BlockSpec(memory_space=pltpu.VMEM)
    smem = pl.BlockSpec(memory_space=pltpu.SMEM)
    hbm = pl.BlockSpec(memory_space=pltpu.HBM)
    bf16, f32 = jnp.bfloat16, jnp.float32
    out, dec, fresh = pl.pallas_call(
        fused_kernel,
        name="attend",
        in_specs=[smem, smem] + [hbm] * 8,
        out_specs=[vmem, vmem, vmem],
        out_shape=[
            pltpu.VMEM((ROWS, LAT), bf16),
            pltpu.VMEM((DROWS, LAT), bf16),
            pltpu.VMEM((2, KVW), bf16),
        ],
        scratch_shapes=[
            pltpu.VMEM((1, LAT), f32),
            pltpu.VMEM((1, 32), jnp.int32),
            pltpu.VMEM((TOK, KVW), bf16),
            pltpu.VMEM((16, KVW), bf16),
            pltpu.VMEM((2, 7168), bf16),
            pltpu.VMEM((112, KVW), bf16),
            pltpu.VMEM((DROWS, KVW), bf16),
            pltpu.VMEM((ROWS, KVW), bf16),
            pltpu.VMEM((KEYS, WIDE), bf16),
            pltpu.VMEM((ROWS + DROWS, WIDE), bf16),
            pltpu.VMEM((ROWS + DROWS, LAT), f32),
            pltpu.VMEM((ROWS + DROWS, 128), f32),
            pltpu.VMEM((ROWS + DROWS, 128), f32),
            pltpu.VMEM((TALL, BROAD), f32),
            pltpu.VMEM((TALL, BROAD), f32),
            pltpu.VMEM((TALL, BROAD), bf16),
            pltpu.VMEM((TALL, BROAD), bf16),
            pltpu.VMEM((7, 8, WIDE), f32),
            pltpu.VMEM((6, 8, WIDE), f32),
            pltpu.SemaphoreType.DMA((SEMS,)),
            pltpu.SemaphoreType.DMA((SEMS,)),
            pltpu.SemaphoreType.DMA((6,)),
            pltpu.SemaphoreType.DMA((6,)),
            pltpu.SemaphoreType.DMA((8,)),
        ],
        compiler_params=pltpu.CompilerParams(
            collective_id=0, has_side_effects=True, vmem_limit_bytes=48 * 2**20
        ),
    )(
        prefix_blocks,
        suffix_len,
        *(
            pltpu.with_memory_space_constraint(array, pltpu.HBM)
            for array in (
                hit_slots,
                suffix_latent[0],
                cache[0, 0],
                decode_hidden[0],
                kv_down,
                decode_query.reshape(DROWS, KVW),
                suffix_query.reshape(ROWS, KVW),
                kv_gain.reshape(1, LAT),
            )
        ),
    )
    out, dec, fresh = pl.pallas_call(
        write_kernel,
        name="write",
        in_specs=[vmem] * 3,
        out_specs=[hbm] * 3,
        out_shape=[
            jax.ShapeDtypeStruct((ROWS, LAT), bf16),
            jax.ShapeDtypeStruct((DROWS, LAT), bf16),
            jax.ShapeDtypeStruct((2, KVW), bf16),
        ],
        scratch_shapes=[pltpu.SemaphoreType.DMA((3,))],
    )(*(pltpu.with_memory_space_constraint(array, pltpu.VMEM) for array in (out, dec, fresh)))
    return (
        out.reshape(1, TOK, HEADS, LAT),
        dec.reshape(1, 2, HEADS, LAT),
        fresh.reshape(1, 2, KVW),
    )


def solution(mesh):
    placed = (
        P("pool", "context", None, None),
        P("pool", None),
        P("pool"),
        P("pool"),
        P("pool", "context", None),
        P("pool", "context", "tensor", None),
        P("pool", None, None),
        P(("context", "tensor"), None),
        P(),
        P("pool", None, "tensor", None),
    )
    return jax.shard_map(
        on_device,
        mesh=mesh,
        in_specs=placed,
        out_specs=(
            P("pool", "context", "tensor", None),
            P("pool", None, "tensor", None),
            P("pool", None, None),
        ),
        check_vma=False,
    )
```

```python
import jax
import jax.numpy as jnp
from jax import lax
from jax.experimental import pallas as pl
from jax.experimental.pallas import tpu as pltpu
from jax.sharding import PartitionSpec as P

SCALE2 = 192.0 ** (-0.5) * 1.4426950408889634
BIG = -1e38
MESH = pl.DeviceIdType.MESH
DIMS = (((1,), (1,)), ((), ()))

NX, NY = 4, 8
TOK, HEADS, KVW, LAT, WIDE = 64, 32, 576, 512, 640
ROWS = TOK * HEADS
DROWS = 2 * HEADS
CHUNK = 80
KEYS = NX * NY * CHUNK

SEGMENTS = (
    (0, 0), (1, 0), (2, 0), (0, 1), (0, 2), (3, 0), (2, 1), (0, 3), (1, 1), (3, 1),
    (2, 2), (0, 4), (1, 2), (1, 3), (2, 3), (1, 4), (3, 3), (2, 4), (3, 4), (3, 2),
)
CARRIER = {(0, 4): 0, (1, 4): 0, (2, 4): 0, (3, 4): 0, (1, 0): 0, (2, 0): 1, (3, 0): 0, (3, 1): 0}


def pair(u):
    return 1 <= u <= 3


def first_chunks():
    place, at = {}, 0
    for g, u in SEGMENTS:
        place[g, u] = at
        at += 2 if pair(u) else 1
    return place


FIRST = first_chunks()
SEM_Y, SEM_X1, SEM_X2, SEM_FAR, SEM_CORE, SEM_SIDE, SEMS = 0, 5, 10, 15, 20, 40, 42

ROW_BLOCKS = ((0, 512), (512, 512), (1024, 512), (1536, 512 + DROWS))
KEY_BLOCKS = ((0, 256), (256, 256), (512, 512), (1024, 512), (1536, 512), (2048, 512))
TALL, BROAD, SUB = 512 + DROWS, 512, 256

SERVICE = {
    (0, 1): (("ready", 2), ("sum",)),
    (0, 3): (("ready", 3), ("near", 1), ("far", 0)),
    (1, 1): (("sum",),),
    (1, 2): (("ready", 4),),
    (2, 0): (("near", 2), ("side",)),
    (2, 2): (("near", 3),),
    (3, 0): (("near", 4), ("sum",)),
    (3, 2): (("far", 2), ("far", 4)),
    (4, 0): (("far", 3),),
    (4, 2): (("sum",),),
    (5, 0): (("sum",),),
}


def needed(block):
    start, width = KEY_BLOCKS[block]
    out = []
    for g, u in SEGMENTS:
        low = FIRST[g, u] * CHUNK
        high = low + (2 if pair(u) else 1) * CHUNK
        if low < start + width and high > start:
            out.append((g, u))
    return out


def fused_kernel(
    prefix_ref,
    slen_ref,
    hits_hbm,
    suffix_hbm,
    cache_hbm,
    hidden_hbm,
    down_hbm,
    dq_hbm,
    q_hbm,
    gain_hbm,
    out_ref,
    dec_ref,
    fresh_ref,
    gain_ref,
    hits_ref,
    suffix_ref,
    cache_ref,
    hidden_ref,
    down_ref,
    dq_ref,
    q_in,
    key_ref,
    qa_ref,
    acc_ref,
    m_ref,
    l_ref,
    s0,
    s1,
    p0,
    p1,
    part_send,
    part_recv,
    send_sem,
    recv_sem,
    psend_sem,
    precv_sem,
    in_sem,
):
    pool = lax.axis_index("pool")
    ctx = lax.axis_index("context")
    core = lax.axis_index("tensor")
    x, y = ctx // NY, ctx % NY

    def chip(dx, dy):
        return (pool, ((x + dx + NX) % NX) * NY + (y + dy + NY) % NY, core)

    sister = (pool, ctx, 1 - core)
    along = 1 - 2 * core
    fold = [
        sister,
        (pool, (x + 1 - 2 * (x % 2)) * NY + y, core),
        (pool, (NX - 1 - x) * NY + y, core),
        (pool, x * NY + y + 1 - 2 * (y % 2), core),
        (pool, x * NY + y + 2 - 4 * ((y // 2) % 2), core),
        chip(0, 4),
    ]
    friends = [sister, chip(1, 0), chip(-1, 0), chip(2, 0), chip(0, 1), chip(0, -1), chip(0, 2), chip(0, -2), chip(0, 4)]
    barrier = pltpu.get_barrier_semaphore()
    for friend in friends:
        pl.semaphore_signal(barrier, inc=1, device_id=friend, device_id_type=MESH)

    loads = (
        (suffix_hbm, suffix_ref),
        (cache_hbm, cache_ref),
        (hits_hbm, hits_ref),
        (hidden_hbm, hidden_ref),
        (down_hbm, down_ref),
        (dq_hbm, dq_ref),
        (q_hbm, q_in),
        (gain_hbm, gain_ref),
    )
    loads = [pltpu.make_async_copy(a, b, in_sem.at[i]) for i, (a, b) in enumerate(loads)]
    for load in loads:
        load.start()

    for load in loads[0:3]:
        load.wait()
    prefix = prefix_ref[0]
    slen = slen_ref[0]
    lane = lax.broadcasted_iota(jnp.int32, (TOK, TOK), 1)
    token = lax.broadcasted_iota(jnp.int32, (TOK, TOK), 0) + ctx * TOK
    hidden_here = ((lane < 32) & (ctx > lane)) | ((lane == 32) & (token >= slen))
    tail = jnp.where(hidden_here, BIG, 0.0).astype(jnp.bfloat16)
    key_ref[0:TOK, :] = jnp.concatenate([suffix_ref[...], tail], axis=1)
    order = lax.broadcasted_iota(jnp.int32, (1, 32), 1)
    hit = jnp.where((hits_ref[...] == ctx) & (order < prefix), 1.0, 0.0)
    live = jnp.max(hit, axis=1, keepdims=True)
    dead = jnp.broadcast_to(jnp.where(live > 0.5, 0.0, BIG), (16, TOK)).astype(jnp.bfloat16)
    key_ref[TOK:CHUNK, :] = jnp.concatenate([cache_ref[...], dead], axis=1)

    pl.semaphore_wait(barrier, len(friends))

    def rows_of(g, u, of_core):
        if pair(u):
            return pl.ds(pl.multiple_of(FIRST[g, u] * CHUNK + of_core * CHUNK, 16), CHUNK)
        return pl.ds(FIRST[g, u] * CHUNK, CHUNK)

    def span(g, u):
        return pl.ds(FIRST[g, u] * CHUNK, 2 * CHUNK if pair(u) else CHUNK)

    def remote(source, target, i, device):
        return pltpu.make_async_remote_copy(
            src_ref=key_ref.at[source],
            dst_ref=key_ref.at[target],
            send_sem=send_sem.at[i],
            recv_sem=recv_sem.at[i],
            device_id=device,
            device_id_type=MESH,
        )

    def y_copy(u):
        source, hops = (rows_of(0, 0, core), u) if u <= 2 else (rows_of(0, u - 2, core), 2)
        return remote(source, rows_of(0, u, core), SEM_Y + u, chip(0, along * hops))

    def near_copy(g, u):
        base = SEM_X1 if g == 1 else SEM_X2
        return remote(rows_of(0, u, core), rows_of(g, u, core), base + u, chip(1 if g == 1 else -1, 0))

    def far_copy(u):
        if u == 0:
            source, hops = rows_of(1, 0, core), 1
        elif u == 2:
            source, hops = rows_of(1, 2, core), 1
        elif u == 3:
            source, hops = rows_of(2, 3, core), -1
        else:
            source, hops = rows_of(0, u, core), 2
        return remote(source, rows_of(3, u, core), SEM_FAR + u, chip(hops, 0))

    def side_copy(way):
        return remote(rows_of(3, 0, core), rows_of(3, 1, way), SEM_SIDE + way, chip(0, 1 - 2 * way))

    def core_copy(g, u, of_core=None):
        if (g, u) in CARRIER or not pair(u):
            rows = span(g, u)
        else:
            rows = rows_of(g, u, core if of_core is None else of_core)
        return remote(rows, rows, SEM_CORE + g * 5 + u, sister)

    def on(which, action):
        if which is None:
            action()
        else:
            pl.when(core == which)(action)

    started = []

    def launch(which, *copies):
        def start():
            for make in copies:
                make().start()

        on(which, start)
        started.append((which, copies))

    def take(g, u, *copies):
        which = CARRIER.get((g, u))

        def wait():
            for make in copies:
                make().wait_recv()

        on(which, wait)
        return which

    def ready(u):
        which = take(0, u, lambda: y_copy(u))
        if u == 1:
            launch(which, lambda: y_copy(3))
        if u == 2:
            launch(0, lambda: y_copy(4))
        launch(which, lambda: near_copy(1, u), lambda: near_copy(2, u))
        if u == 4:
            launch(which, lambda: far_copy(u))
        launch(which, lambda: core_copy(0, u))

    def near(u):
        for g in (1, 2):
            which = take(g, u, lambda g=g: near_copy(g, u))
            if (u, g) in ((0, 1), (2, 1), (3, 2)):
                launch(which, lambda: far_copy(u))
            launch(which, lambda g=g: core_copy(g, u))

    def far(u):
        which = take(3, u, lambda: far_copy(u))
        if u == 0:
            launch(which, lambda: side_copy(0), lambda: side_copy(1))
        launch(which, lambda: core_copy(3, u))

    def side():
        which = take(3, 1, lambda: side_copy(0), lambda: side_copy(1))
        launch(which, lambda: core_copy(3, 1))

    def fold_copy(i):
        return pltpu.make_async_remote_copy(
            src_ref=part_send.at[i],
            dst_ref=part_recv.at[i],
            send_sem=psend_sem.at[i],
            recv_sem=precv_sem.at[i],
            device_id=fold[i],
            device_id_type=MESH,
        )

    def fold_step(i):
        if i > 0:
            fold_copy(i - 1).wait_recv()
            part_send[i] = part_send[i - 1] + part_recv[i - 1]
        if i < 6:
            fold_copy(i).start()

    sums = [0]
    arrived = {(0, 0)}
    served = {(0, 0)}

    def serve(event):
        kind = event[0]
        if kind == "sum":
            fold_step(sums[0])
            sums[0] += 1
        elif kind == "ready":
            ready(event[1])
            served.add((0, event[1]))
        elif kind == "near":
            near(event[1])
            served.update({(1, event[1]), (2, event[1])})
        elif kind == "far":
            far(event[1])
            served.add((3, event[1]))
        else:
            side()
            served.add((3, 1))

    def from_sister(g, u):
        which = CARRIER.get((g, u))
        on(None if which is None else 1 - which, lambda: core_copy(g, u, 1 - core).wait_recv())

    def await_block(block):
        for segment in needed(block):
            if segment not in arrived:
                assert segment in served, segment
                from_sister(*segment)
                arrived.add(segment)

    units = [(k, r) for k in range(len(KEY_BLOCKS)) for r in range(len(ROW_BLOCKS))]
    score, weight = [s0, s1], [p0, p1]
    last = len(KEY_BLOCKS) - 1

    def wide(state, lanes):
        return jnp.concatenate([state] * (lanes // 128), axis=1)

    def scores(i, j):
        k, r = units[i]
        start, n = ROW_BLOCKS[r]
        low = KEY_BLOCKS[k][0] + j * SUB
        s = lax.dot_general(qa_ref[start : start + n, :], key_ref[low : low + SUB, :], DIMS, preferred_element_type=jnp.float32)
        if low == 0:
            row = lax.broadcasted_iota(jnp.int32, (n, 128), 0)
            col = lax.broadcasted_iota(jnp.int32, (n, 128), 1)
            tok = (row + start) // HEADS
            mask = (col < TOK) & (col > tok) & (tok < TOK)
            score[i % 2][0:n, 0:128] = jnp.where(mask, BIG, s[:, 0:128])
            score[i % 2][0:n, 128:SUB] = s[:, 128:]
        else:
            score[i % 2][0:n, j * SUB : (j + 1) * SUB] = s

    def subs(i):
        return range(KEY_BLOCKS[units[i][0]][1] // SUB)

    def row_max(i):
        k, r = units[i]
        start, n = ROW_BLOCKS[r]
        top = jnp.max(score[i % 2][0:n, 0 : KEY_BLOCKS[k][1]], axis=1, keepdims=True) * SCALE2
        top = jnp.broadcast_to(top, (n, 128))
        if k == 0:
            m_ref[start : start + n] = top
            return None
        old = m_ref[start : start + n]
        new = jnp.maximum(old, top)
        m_ref[start : start + n] = new
        return jnp.exp2(old - new)

    def soft(i, j, total):
        k, r = units[i]
        start, n = ROW_BLOCKS[r]
        s = score[i % 2][0:n, j * SUB : (j + 1) * SUB]
        p = jnp.exp2(s * SCALE2 - wide(m_ref[start : start + n], SUB))
        weight[i % 2][0:n, j * SUB : (j + 1) * SUB] = p.astype(jnp.bfloat16)
        for c in range(0, SUB, 128):
            total = p[:, c : c + 128] if total is None else total + p[:, c : c + 128]
        return total

    def fresh_rows():
        raw = part_send[6]
        latent = raw[:, 0:LAT]
        norm = latent * lax.rsqrt(jnp.sum(latent * latent, axis=1, keepdims=True) * (1.0 / LAT) + 1e-06) * gain_ref[...]
        rope = raw[:, LAT:WIDE]
        lanes = lax.broadcasted_iota(jnp.int32, (8, 128), 1)
        step = lax.broadcasted_iota(jnp.int32, (8, 128), 0)
        pos = (prefix * 16 + slen + step).astype(jnp.float32)
        freq = jnp.exp((lanes % 32).astype(jnp.float32) * (-9.210340371976184 / 32.0))
        angle = pos * freq
        cosine, sine = jnp.cos(angle), jnp.sin(angle)
        ahead = pltpu.roll(rope, 96, 1)
        behind = pltpu.roll(rope, 32, 1)
        turned = jnp.where(lanes < 32, rope * cosine - ahead * sine, rope * cosine + behind * sine)
        turned = jnp.where(lanes < 64, turned, 0.0)
        return jnp.concatenate([norm, turned], axis=1).astype(jnp.bfloat16)

    def decode_end(acc, total):
        fresh = fresh_rows()
        fresh_ref[...] = fresh[0:2, 0:KVW]
        sf = lax.dot_general(qa_ref[ROWS : ROWS + DROWS, :], fresh, DIMS, preferred_element_type=jnp.float32) * SCALE2
        row = lax.broadcasted_iota(jnp.int32, (DROWS, 8), 0) // HEADS
        col = lax.broadcasted_iota(jnp.int32, (DROWS, 8), 1)
        sf = jnp.where(col <= row, sf, BIG)
        old = m_ref[ROWS : ROWS + DROWS, 0:1]
        new = jnp.maximum(old, jnp.max(sf, axis=1, keepdims=True))
        pf = jnp.exp2(sf - new)
        fade = jnp.exp2(old - new)
        total = total * fade + jnp.sum(pf, axis=1, keepdims=True)
        more = jnp.dot(pf.astype(jnp.bfloat16), fresh[:, 0:LAT], preferred_element_type=jnp.float32)
        dec_ref[...] = ((acc * fade + more) / total).astype(jnp.bfloat16)

    def context(i, total, fade):
        k, r = units[i]
        start, n = ROW_BLOCKS[r]
        low, width = KEY_BLOCKS[k]
        o = jnp.dot(weight[i % 2][0:n, 0:width], key_ref[low : low + width, 0:LAT], preferred_element_type=jnp.float32)
        here = slice(start, start + n)
        if k > 0:
            total = l_ref[here] * fade + total
            o = acc_ref[here] * wide(fade, LAT) + o
        if k < last:
            l_ref[here] = total
            acc_ref[here] = o
            return
        end = min(start + n, ROWS) - start
        total = jnp.sum(total, axis=1, keepdims=True)
        over = jnp.broadcast_to(1.0 / total[0:end], (end, 128))
        out_ref[start : start + end, :] = (o[0:end] * wide(over, LAT)).astype(jnp.bfloat16)
        if end < n:
            decode_end(o[end:n], total[end:n])

    y_copy(1).start()
    launch(0, lambda: near_copy(1, 0))
    launch(1, lambda: near_copy(2, 0))

    for load in loads[3:5]:
        load.wait()
    part = ctx * 2 + core
    lane_block = jnp.minimum((part * 112) // 128, 54)
    shift = part * 112 - lane_block * 128
    window = hidden_ref[:, pl.ds(pl.multiple_of(lane_block * 128, 128), 256)]
    pick = lax.broadcasted_iota(jnp.int32, (256, 112), 0) == lax.broadcasted_iota(jnp.int32, (256, 112), 1) + shift
    pick = jnp.where(pick, 1.0, 0.0).astype(jnp.bfloat16)
    piece = jnp.dot(window, pick, preferred_element_type=jnp.float32).astype(jnp.bfloat16)
    partial = jnp.dot(piece, down_ref[...], preferred_element_type=jnp.float32)
    part_send[...] = jnp.zeros_like(part_send)
    part_send[0, 0:2, 0:KVW] = partial
    y_copy(1).wait_send()
    launch(None, lambda: y_copy(2))
    serve(("sum",))

    for load in loads[5:]:
        load.wait()
    lanes = lax.broadcasted_iota(jnp.int32, (256, TOK), 1)
    pick_rank = jnp.where(lanes == ctx, 1.0, 0.0).astype(jnp.bfloat16)

    def widen(i, carry):
        rows = pl.ds(pl.multiple_of(i * 256, 256), 256)
        qa_ref[rows, :] = jnp.concatenate([q_in[rows, :], pick_rank], axis=1)
        return carry

    lax.fori_loop(0, ROWS // 256, widen, 0)
    pick_dec = jnp.where(lanes[0:DROWS] == 32, 1.0, 0.0).astype(jnp.bfloat16)
    qa_ref[ROWS : ROWS + DROWS, :] = jnp.concatenate([dq_ref[...], pick_dec], axis=1)

    for event in (("ready", 1), ("near", 0), ("sum",)):
        serve(event)

    await_block(0)
    for j in subs(0):
        scores(0, j)
    fade = row_max(0)
    for i, unit in enumerate(units):
        more = i + 1 < len(units)
        if more and units[i + 1][0] != unit[0]:
            await_block(units[i + 1][0])
        total = None
        ahead = list(subs(i + 1)) if more else []
        for j in range(max(len(ahead), len(subs(i)))):
            if j < len(ahead):
                scores(i + 1, j)
            if j < len(subs(i)):
                total = soft(i, j, total)
        context(i, total, fade)
        if more:
            fade = row_max(i + 1)
        for event in SERVICE.get(unit, ()):
            serve(event)

    assert sums[0] == 7
    for which, copies in started:

        def sent(copies=copies):
            for make in copies:
                make().wait_send()

        on(which, sent)
    for i in range(6):
        fold_copy(i).wait_send()


def write_kernel(out_vmem, dec_vmem, fresh_vmem, out_ref, dec_ref, fresh_ref, sem):
    copies = ((out_vmem, out_ref), (dec_vmem, dec_ref), (fresh_vmem, fresh_ref))
    copies = [pltpu.make_async_copy(a, b, sem.at[i]) for i, (a, b) in enumerate(copies)]
    for copy in copies:
        copy.start()
    for copy in copies:
        copy.wait()


def on_device(
    cache,
    hit_slots,
    prefix_blocks,
    suffix_len,
    suffix_latent,
    suffix_query,
    decode_hidden,
    kv_down,
    kv_gain,
    decode_query,
):
    vmem = pl.BlockSpec(memory_space=pltpu.VMEM)
    smem = pl.BlockSpec(memory_space=pltpu.SMEM)
    hbm = pl.BlockSpec(memory_space=pltpu.HBM)
    bf16, f32 = jnp.bfloat16, jnp.float32
    out, dec, fresh = pl.pallas_call(
        fused_kernel,
        name="attend",
        in_specs=[smem, smem] + [hbm] * 8,
        out_specs=[vmem, vmem, vmem],
        out_shape=[
            pltpu.VMEM((ROWS, LAT), bf16),
            pltpu.VMEM((DROWS, LAT), bf16),
            pltpu.VMEM((2, KVW), bf16),
        ],
        scratch_shapes=[
            pltpu.VMEM((1, LAT), f32),
            pltpu.VMEM((1, 32), jnp.int32),
            pltpu.VMEM((TOK, KVW), bf16),
            pltpu.VMEM((16, KVW), bf16),
            pltpu.VMEM((2, 7168), bf16),
            pltpu.VMEM((112, KVW), bf16),
            pltpu.VMEM((DROWS, KVW), bf16),
            pltpu.VMEM((ROWS, KVW), bf16),
            pltpu.VMEM((KEYS, WIDE), bf16),
            pltpu.VMEM((ROWS + DROWS, WIDE), bf16),
            pltpu.VMEM((ROWS + DROWS, LAT), f32),
            pltpu.VMEM((ROWS + DROWS, 128), f32),
            pltpu.VMEM((ROWS + DROWS, 128), f32),
            pltpu.VMEM((TALL, BROAD), f32),
            pltpu.VMEM((TALL, BROAD), f32),
            pltpu.VMEM((TALL, BROAD), bf16),
            pltpu.VMEM((TALL, BROAD), bf16),
            pltpu.VMEM((7, 8, WIDE), f32),
            pltpu.VMEM((6, 8, WIDE), f32),
            pltpu.SemaphoreType.DMA((SEMS,)),
            pltpu.SemaphoreType.DMA((SEMS,)),
            pltpu.SemaphoreType.DMA((6,)),
            pltpu.SemaphoreType.DMA((6,)),
            pltpu.SemaphoreType.DMA((8,)),
        ],
        compiler_params=pltpu.CompilerParams(
            collective_id=0, has_side_effects=True, vmem_limit_bytes=48 * 2**20
        ),
    )(
        prefix_blocks,
        suffix_len,
        *(
            pltpu.with_memory_space_constraint(array, pltpu.HBM)
            for array in (
                hit_slots,
                suffix_latent[0],
                cache[0, 0],
                decode_hidden[0],
                kv_down,
                decode_query.reshape(DROWS, KVW),
                suffix_query.reshape(ROWS, KVW),
                kv_gain.reshape(1, LAT),
            )
        ),
    )
    out, dec, fresh = pl.pallas_call(
        write_kernel,
        name="write",
        in_specs=[vmem] * 3,
        out_specs=[hbm] * 3,
        out_shape=[
            jax.ShapeDtypeStruct((ROWS, LAT), bf16),
            jax.ShapeDtypeStruct((DROWS, LAT), bf16),
            jax.ShapeDtypeStruct((2, KVW), bf16),
        ],
        scratch_shapes=[pltpu.SemaphoreType.DMA((3,))],
    )(*(pltpu.with_memory_space_constraint(array, pltpu.VMEM) for array in (out, dec, fresh)))
    return (
        out.reshape(1, TOK, HEADS, LAT),
        dec.reshape(1, 2, HEADS, LAT),
        fresh.reshape(1, 2, KVW),
    )


def solution(mesh):
    placed = (
        P("pool", "context", None, None),
        P("pool", None),
        P("pool"),
        P("pool"),
        P("pool", "context", None),
        P("pool", "context", "tensor", None),
        P("pool", None, None),
        P(("context", "tensor"), None),
        P(),
        P("pool", None, "tensor", None),
    )
    return jax.shard_map(
        on_device,
        mesh=mesh,
        in_specs=placed,
        out_specs=(
            P("pool", "context", "tensor", None),
            P("pool", None, "tensor", None),
            P("pool", None, None),
        ),
        check_vma=False,
    )
```
